32 devices in a mesh: gx: 8 (over z, x), gy: 4 (over y, core).
Axes of the slice: x: 2, y: 2, z: 4, core: 2. Of those that a mesh axis runs over, the one named last changes fastest.
Arguments:
- features: bfloat16 [16384, 128], P(('gx', 'gy')), may hold values from -6 to 6
- cotangent: bfloat16 [16384, 128], P(('gx', 'gy')), may hold values from -6 to 6
- block_pos: int32 [256], P(('gx', 'gy')), may hold values from -1 to 11, as said below
- weight_one: bfloat16 [3456, 128], replicated, may hold values from -0.1875 to 0.1875
- weight_two: bfloat16 [3456, 128], replicated, may hold values from -0.1875 to 0.1875
Outputs:
- output: bfloat16 [16384, 128], P(('gx', 'gy'))
- input_grad: float32 [16384, 128], P(('gx', 'gy'))
- grad_one: float32 [3456, 128], replicated
- grad_two: float32 [3456, 128], replicated
The draws below stay inside these ranges and needn't reach their ends.
Inputs may be any that keep to these rules, and one draw needn't show every extreme that they name: `block_pos`: local position p numbers a device's 2 x 2 x 3 block grid as (bx * 2 + by) * 3 + bz. A device's used slots come first and hold distinct positions, the rest hold -1; every device uses 2 or more slots and some device uses all 8.
All inputs are finite; a program needn't handle non-finite values.
Results may differ from the reference program's by a relative error of at most 0.0043.
Values may be sent and summed in bfloat16 or wider, within the bound.
A program may use at most 128 MiB of HBM per device.

```python
import jax
import jax.numpy as jnp
from jax import lax

C = 128
LBX = 2
LBY = 2
LBZ = 3
POS = 12
NB = 8
NBX = 16
NBY = 8
ROWS = 16384
N_GX = 8
N_GY = 4


def draw_block_pos(key, part):
    dev_count = N_GX * N_GY
    perm_key, count_key, full_key = jax.random.split(key, 3)
    orders = jax.vmap(lambda sub_key: jax.random.permutation(sub_key, POS))(jax.random.split(perm_key, dev_count))
    orders = orders.astype(jnp.int32)
    counts = jax.random.randint(count_key, (dev_count,), NB // 4, NB + 1)
    fullest = jax.random.randint(full_key, (), 0, dev_count)
    devices = jnp.arange(dev_count)
    counts = jnp.where(devices == fullest, NB, counts)
    first_at = jnp.argmax(orders == POS - 1, axis=1).astype(jnp.int32)
    rolled = jnp.take_along_axis(orders, (jnp.arange(POS, dtype=jnp.int32)[None, :] + first_at[:, None]) % POS, axis=1)
    orders = jnp.where((devices == fullest)[:, None], rolled, orders)
    chosen = jnp.where(jnp.arange(NB)[None, :] < counts[:, None], orders[:, :NB], -1)
    return chosen.reshape(-1).astype(jnp.int32)


def shard_levels(stream_key, dims, cuts, smallest, top_value):
    loudness = 1.0
    for dim, shards_of in cuts:
        steps = jax.random.uniform(jax.random.fold_in(jax.random.fold_in(stream_key, 6), dim), (shards_of,), jnp.float32, smallest / len(cuts), top_value / len(cuts))
        loudness = loudness * jnp.repeat(jnp.exp(steps), dims[dim] // shards_of).reshape((-1,) + (1,) * (len(dims) - 1 - dim))
    return loudness


def bell_draw(stream_key, dims, deviation, limit, cuts=(), kind=jnp.bfloat16):
    array = deviation * jax.random.normal(stream_key, dims, jnp.float32)
    if cuts:
        array = array * shard_levels(stream_key, dims, cuts, -0.22, 0.18)
    return jnp.clip(array, -limit, limit).astype(kind)


def setup_inputs(seed: int = 0) -> dict:
    key_of = jax.random.split(jax.random.key(seed), 6)
    return {
        "features": bell_draw(key_of[0], (ROWS, C), 1.0, 6.0, ((0, 32),)),
        "cotangent": bell_draw(key_of[1], (ROWS, C), 1.0, 6.0, ((0, 32),)),
        "block_pos": draw_block_pos(jax.random.fold_in(key_of[5], 71), 0),
        "weight_one": bell_draw(key_of[3], (27 * C, C), (9 * C) ** -0.5, 0.1875),
        "weight_two": bell_draw(key_of[4], (27 * C, C), (9 * C) ** -0.5, 0.1875),
    }


def flipped(weight):
    width = weight.shape[1]
    return weight.reshape(27, width, width)[::-1].transpose(0, 2, 1).reshape(27 * width, width)

def columns_of(padded, corner_x, corner_y, corner_z):
    chan_width = padded.shape[3]

    def window(start_x, start_y, start_z):
        starts = (start_x.astype(jnp.int32), start_y.astype(jnp.int32), start_z.astype(jnp.int32), jnp.zeros((), jnp.int32))
        return lax.dynamic_slice(padded, starts, (6, 6, 6, chan_width))
    windows = jax.vmap(window)(corner_x, corner_y, corner_z)
    pieces = [windows[:, off_x:off_x + 4, off_y:off_y + 4, off_z:off_z + 4] for off_x in range(3) for off_y in range(3) for off_z in range(3)]
    stacked = jnp.stack(pieces, axis=4)
    return stacked.reshape(windows.shape[0] * 64, 27 * chan_width)

def reference(features, cotangent, block_pos, weight_one, weight_two):
    chan_width = features.shape[1]
    dev_count = N_GX * N_GY
    active = block_pos >= 0
    row_mask = jnp.repeat(active, 64)[:, None]
    slot_ids = jnp.arange(dev_count * NB, dtype=jnp.int32)
    device = slot_ids // NB
    index_x = device // N_GY
    index_y = device % N_GY
    position = jnp.where(active, block_pos, 0).astype(jnp.int32)
    block_x = index_x * LBX + position // (LBY * LBZ)
    block_y = index_y * LBY + position // LBZ % LBY
    block_z = position % LBZ
    flat = jnp.where(active, (block_x * NBY + block_y) * LBZ + block_z, NBX * NBY * LBZ).astype(jnp.int32)
    corner_x = (block_x * 4).astype(jnp.int32).reshape(dev_count, NB)
    corner_y = (block_y * 4).astype(jnp.int32).reshape(dev_count, NB)
    corner_z = (block_z * 4).astype(jnp.int32).reshape(dev_count, NB)

    def to_dense(values):
        blocks = jnp.zeros((NBX * NBY * LBZ, 64 * chan_width), values.dtype)
        blocks = blocks.at[flat].set(values.reshape(-1, 64 * chan_width), mode='drop')
        blocks = blocks.reshape(NBX, NBY, LBZ, 4, 4, 4, chan_width).transpose(0, 3, 1, 4, 2, 5, 6)
        dense = blocks.reshape(NBX * 4, NBY * 4, LBZ * 4, chan_width)
        return jnp.pad(dense, ((1, 1), (1, 1), (1, 1), (0, 0)))

    def conv_all(values, weight):
        padded = to_dense(values)

        def per_device(corners):
            cols = columns_of(padded, corners[0], corners[1], corners[2])
            return jnp.dot(cols, weight, preferred_element_type=jnp.float32)
        result = lax.map(per_device, (corner_x, corner_y, corner_z))
        return result.reshape(-1, chan_width)

    def gram_all(values, grads):
        padded = to_dense(values)
        grads_dev = grads.reshape(dev_count, NB * 64, chan_width)

        def step_fn(carry, item):
            corners_x, corners_y, corners_z, grad_rows = item
            cols = columns_of(padded, corners_x, corners_y, corners_z)
            term = lax.dot_general(cols, grad_rows, (((0,), (0,)), ((), ())), preferred_element_type=jnp.float32)
            return (carry + term, None)
        start = jnp.zeros((27 * chan_width, chan_width), jnp.float32)
        total, _ = lax.scan(step_fn, start, (corner_x, corner_y, corner_z, grads_dev))
        return total / jnp.sqrt(jnp.float32(ROWS))
    x_in = jnp.where(row_mask, features, 0).astype(jnp.bfloat16)
    pre_one = conv_all(x_in, weight_one)
    sigmoid_one = jax.nn.sigmoid(pre_one)
    hidden = jnp.where(row_mask, pre_one * sigmoid_one, 0.0).astype(jnp.bfloat16)
    pre_two = conv_all(hidden, weight_two)
    output = jnp.where(row_mask, pre_two + x_in.astype(jnp.float32), 0.0).astype(jnp.bfloat16)
    upstream = jnp.where(row_mask, cotangent, 0).astype(jnp.bfloat16)
    back_two = conv_all(upstream, flipped(weight_two))
    slope = sigmoid_one * (1.0 + pre_one * (1.0 - sigmoid_one))
    hidden_grad = jnp.where(row_mask, back_two * slope, 0.0).astype(jnp.bfloat16)
    back_one = conv_all(hidden_grad, flipped(weight_one))
    input_grad = jnp.where(row_mask, upstream.astype(jnp.float32) + back_one, 0.0).astype(jnp.float32)
    grad_two = gram_all(hidden, upstream)
    grad_one = gram_all(x_in, hidden_grad)
    return (output, input_grad, grad_one, grad_two)
```

```python
import functools

import jax
import jax.numpy as jnp
import numpy as np
from jax import lax
from jax.experimental import pallas as pl
from jax.experimental.pallas import tpu as pltpu
from jax.sharding import PartitionSpec as P

PLANE = 96
GRID = 768
EXT = 960
C = 128
TAPS = 9 * C
MESH = pl.DeviceIdType.MESH
BF = jnp.bfloat16
F32 = jnp.float32


def face_matrix():
    out = np.zeros((256, GRID), np.float32)
    for side, y in ((0, 0), (1, 7)):
        for x in range(8):
            for z in range(12):
                out[side * 128 + x * 16 + z, x * PLANE + z * 8 + y] = 1
    return out


def spread_matrix():
    out = np.zeros((2, EXT, 160), np.float32)
    for side, y in ((0, 0), (1, 7)):
        for x in range(10):
            for z in range(12):
                out[side, x * PLANE + z * 8 + y, x * 16 + z] = 1
    return out


def dot(a, b):
    return jnp.dot(a, b, preferred_element_type=F32)


def dot_nt(a, b):
    return lax.dot_general(a, b, (((1,), (1,)), ((), ())), preferred_element_type=F32)


def kernel(n_gx, n_gy, rz, feat, cot, trow, tcol, w1, w2, face, spread,
           out_ref, ig_ref, grad_ref,
           gp, yf, xr, yr, fx, fu, fh, fg, wt1, wt2, acc, send_c, recv_c, s1b, recv_p,
           s2f, s2b, recv_z, gat,
           ex_s, ex_r, c_s, c_r, p_s, p_r, z_s, z_r, az_s, az_r, ap_s, ap_r, ac_s, ac_r):
    i = lax.axis_index("gx")
    j = lax.axis_index("gy")
    n3 = n_gx // 2
    ny = n_gy // 2
    np_ = 2 * ny
    half = acc.shape[1] // 2
    quarter = half // np_
    pad = rz * n3
    core = lax.rem(j, 2)
    xb = lax.rem(i, 2)
    yb = j // 2
    me_p = yb * 2 + xb
    k = i // 2

    def shift(di, dj):
        return (lax.rem(i + di + n_gx, n_gx), lax.rem(j + dj + n_gy, n_gy))

    def plane_peer(r):
        rx, ry = r % 2, r // 2
        px = lax.rem(xb + rx, 2)
        py = lax.rem(yb + ry, ny)
        return (k * 2 + px, py * 2 + core), py * 2 + px

    def z_peer(d):
        pk = lax.rem(k + d, n3)
        return (pk * 2 + xb, j), pk

    other = (i, yb * 2 + (1 - core))
    dirs = [(a, b) for a in (-1, 0, 1) for b in (-1, 0, 1) if (a, b) != (0, 0)]

    barrier = pltpu.get_barrier_semaphore()
    targets = [shift(a, b) for a, b in dirs] + [other]
    targets += [plane_peer(r)[0] for r in range(1, np_)]
    targets += [z_peer(d)[0] for d in range(1, n3)]
    for t in targets:
        pl.semaphore_signal(barrier, inc=1, device_id=t, device_id_type=MESH)

    def remote(src, dst, ss, rs, dev):
        c = pltpu.make_async_remote_copy(src_ref=src, dst_ref=dst, send_sem=ss, recv_sem=rs,
                                         device_id=dev, device_id_type=MESH)
        c.start()
        return c

    place = jnp.where(lax.broadcasted_iota(jnp.int32, (GRID, 512), 0) == trow[...], 1.0, 0.0)
    place = place.astype(BF)
    xg = dot(place, feat[...])
    ug = dot(place, cot[...])
    mask = dot(place, jnp.ones((512, C), BF))

    def put(e, a, b):
        gp[e, :, 0:C] = a.astype(BF)
        gp[e, :, C:2 * C] = b.astype(BF)
        yf[e] = dot(face[...], gp[e]).astype(BF)

    def exchange(e):
        copies = []
        for n, (a, b) in enumerate(dirs):
            if b == 0:
                src = gp.at[e, pl.ds(0 if a < 0 else GRID - PLANE, PLANE)]
                dst = xr.at[e, 1 if a < 0 else 0]
            else:
                base = 0 if b < 0 else 128
                side = 1 if b < 0 else 0
                if a == 0:
                    src = yf.at[e, pl.ds(base, 128)]
                    dst = yr.at[e, side, pl.ds(16, 128)]
                else:
                    src = yf.at[e, pl.ds(base + (0 if a < 0 else 112), 16)]
                    dst = yr.at[e, side, pl.ds(144 if a < 0 else 0, 16)]
            copies.append(remote(src, dst, ex_s.at[e, n], ex_r.at[e, n], shift(a, b)))
        return copies

    one = jnp.float32(1.0)
    zero = jnp.float32(0.0)
    lo_x = jnp.where(i > 0, one, zero)
    hi_x = jnp.where(i < n_gx - 1, one, zero)
    lo_y = jnp.where(j > 0, one, zero)
    hi_y = jnp.where(j < n_gy - 1, one, zero)

    def expanded(e):
        row = lax.broadcasted_iota(jnp.int32, (160, 2 * C), 0)
        edge = jnp.where(row < 16, lo_x, jnp.where(row >= 144, hi_x, one))
        ylo = (yr[e, 0].astype(F32) * (edge * lo_y)).astype(BF)
        yhi = (yr[e, 1].astype(F32) * (edge * hi_y)).astype(BF)
        return (xr[e, 0].astype(F32) * lo_x, xr[e, 1].astype(F32) * hi_x,
                dot(spread[0], ylo), dot(spread[1], yhi))

    def build(dst, e, f, halo):
        lanes = slice(f * C, (f + 1) * C)
        xlo, xhi, ylo, yhi = (h[:, lanes] for h in halo)
        ext = jnp.concatenate([xlo, gp[e, :, lanes].astype(F32), xhi], axis=0)
        ypos = lax.rem(lax.broadcasted_iota(jnp.int32, (EXT, C), 0), 8)
        below = jnp.where(ypos == 0, ylo, pltpu.roll(ext, 1, 0))
        above = jnp.where(ypos == 7, yhi, pltpu.roll(ext, EXT - 1, 0))
        blank = jnp.zeros((10, 8, C), F32)
        for dy, v in enumerate((below, ext, above)):
            v = v.reshape(10, PLANE, C)
            forms = (jnp.concatenate([blank, v[:, :PLANE - 8]], axis=1), v,
                     jnp.concatenate([v[:, 8:], blank], axis=1))
            for dz, w in enumerate(forms):
                o = (3 * dy + dz) * C
                dst[:, o:o + C] = w.reshape(EXT, C).astype(BF)

    def conv(f9, w):
        total = None
        for dx in range(3):
            t = dot(f9[dx * PLANE:dx * PLANE + GRID, :], w[dx * TAPS:(dx + 1) * TAPS, :])
            total = t if total is None else total + t
        return total

    def conv_t(f9, wt):
        total = None
        for dx in range(3):
            t = dot_nt(f9[dx * PLANE:dx * PLANE + GRID, :], wt[:, dx * TAPS:(dx + 1) * TAPS])
            total = t if total is None else total + t
        return total

    def gram(g, left, f9):
        for dx in range(3):
            t = dot(left, f9[dx * PLANE:dx * PLANE + GRID, :])
            for q in range(9):
                o = 26 - (9 * dx + q)
                acc[g, o * C:(o + 1) * C, :] = t[:, q * C:(q + 1) * C]

    put(0, xg, ug)
    pl.semaphore_wait(barrier, len(targets))
    pending = []
    ex = exchange(0)
    for o in range(27):
        lanes = slice(o * C, (o + 1) * C)
        rows = slice((26 - o) * C, (27 - o) * C)
        wt1[:, lanes] = w1[rows, :]
        wt2[:, lanes] = w2[rows, :]
    x_t = jnp.transpose(xg).astype(BF)
    for c in ex:
        c.wait_recv()
    pending += ex
    halo = expanded(0)
    build(fx, 0, 0, halo)
    build(fu, 0, 1, halo)

    pre = conv(fx, w1)
    sig = jax.nn.sigmoid(pre)
    hidden = pre * sig * mask
    back = conv_t(fu, wt2)
    hgrad = back * (sig * (1.0 + pre * (1.0 - sig))) * mask
    put(1, hidden, hgrad)
    ex = exchange(1)
    pending += ex

    def core_start(g):
        send_c[g] = acc[g, pl.ds(pl.multiple_of((1 - core) * half, 16), half), :].astype(BF)
        return remote(send_c.at[g], recv_c.at[g], c_s.at[g], c_r.at[g], other)

    def plane_start(g, c):
        c.wait_recv()
        own = acc[g, pl.ds(pl.multiple_of(core * half, 16), half), :] + recv_c[g].astype(F32)
        s1b[g] = own.astype(BF)
        acc[g, pl.ds(pl.multiple_of(core * half, 16), half), :] = own
        copies = []
        for r in range(1, np_):
            dev, pq = plane_peer(r)
            copies.append(remote(s1b.at[g, pl.ds(pl.multiple_of(pq * quarter, 16), quarter)],
                                 recv_p.at[g, r - 1], p_s.at[g, r - 1], p_r.at[g, r - 1], dev))
        return copies

    def z_start(g, cs):
        for c in cs:
            c.wait_recv()
        at = pl.multiple_of(core * half + me_p * quarter, 16)
        own = acc[g, pl.ds(at, quarter), :]
        for r in range(np_ - 1):
            own = own + recv_p[g, r].astype(F32)
        if pad > quarter:
            own = jnp.concatenate([own, jnp.zeros((pad - quarter, C), F32)], axis=0)
        s2f[g] = own
        s2b[g] = own.astype(BF)
        copies = []
        for d in range(1, n3):
            dev, pk = z_peer(d)
            copies.append(remote(s2b.at[g, pl.ds(pl.multiple_of(pk * rz, 16), rz)],
                                 recv_z.at[g, d - 1], z_s.at[g, d - 1], z_r.at[g, d - 1], dev))
        return copies

    def gather_z(g, cs):
        for c in cs:
            c.wait_recv()
        own = s2f[g, pl.ds(pl.multiple_of(k * rz, 16), rz), :]
        for d in range(n3 - 1):
            own = own + recv_z[g, d].astype(F32)
        at = pl.multiple_of((core * np_ + me_p) * pad + k * rz, 16)
        gat[g, pl.ds(at, rz), :] = own.astype(BF)
        block = gat.at[g, pl.ds(at, rz)]
        return [remote(block, block, az_s.at[g, d - 1], az_r.at[g, d - 1], z_peer(d)[0])
                for d in range(1, n3)]

    def gather_plane(g, cs):
        for c in cs:
            c.wait_recv()
        block = gat.at[g, pl.ds(pl.multiple_of((core * np_ + me_p) * pad, 16), pad)]
        return [remote(block, block, ap_s.at[g, r - 1], ap_r.at[g, r - 1], plane_peer(r)[0])
                for r in range(1, np_)]

    def gather_core(g, cs):
        for c in cs:
            c.wait_recv()
        block = gat.at[g, pl.ds(pl.multiple_of(core * np_ * pad, 16), np_ * pad)]
        return [remote(block, block, ac_s.at[g], ac_r.at[g], other)]

    h_t = jnp.transpose(hidden).astype(BF)
    gram(0, h_t, fu)
    c0 = core_start(0)
    for c in ex:
        c.wait_recv()
    halo = expanded(1)
    build(fg, 1, 1, halo)
    p0 = plane_start(0, c0)
    gram(1, x_t, fg)
    c1 = core_start(1)
    build(fh, 1, 0, halo)
    p1 = plane_start(1, c1)
    pre_two = conv(fh, w2)
    pick = jnp.where(lax.broadcasted_iota(jnp.int32, (512, GRID), 1) == tcol[...], 1.0, 0.0)
    pick = pick.astype(BF)
    og = (pre_two + gp[0, :, 0:C].astype(F32)).astype(BF)
    out_ref[...] = dot(pick, og).astype(BF)
    z0 = z_start(0, p0)
    ig = conv_t(fg, wt1) + gp[0, :, C:2 * C].astype(F32)
    ig_hi = ig.astype(BF)
    ig_lo = (ig - ig_hi.astype(F32)).astype(BF)
    ig_ref[...] = dot(pick, ig_hi) + dot(pick, ig_lo)
    z1 = z_start(1, p1)
    a0 = gather_z(0, z0)
    a1 = gather_z(1, z1)
    b0 = gather_plane(0, a0)
    b1 = gather_plane(1, a1)
    d0 = gather_core(0, b0)
    d1 = gather_core(1, b1)
    for g, cs in ((0, d0), (1, d1)):
        for c in cs:
            c.wait_recv()
        for q in range(2 * np_):
            grad_ref[g, q * quarter:(q + 1) * quarter, :] = gat[g, q * pad:q * pad + quarter, :]
    for c in pending + [c0, c1] + p0 + p1 + z0 + z1 + a0 + a1 + b0 + b1 + d0 + d1:
        c.wait_send()


def per_device(n_gx, n_gy, features, cotangent, block_pos, weight_one, weight_two):
    rows = features.shape[0]
    n3 = n_gx // 2
    np_ = n_gy
    taps = weight_one.shape[0]
    half = taps // 2
    quarter = half // np_
    rz = -(-quarter // (16 * n3)) * 16
    pad = rz * n3
    v = jnp.arange(64, dtype=jnp.int32)
    inner = v // 16 * PLANE + v % 4 * 8 + v // 4 % 4
    p = block_pos
    corner = p // 6 * 4 * PLANE + p % 3 * 32 + p // 3 % 2 * 4
    target = jnp.where(p[:, None] >= 0, corner[:, None] + inner[None, :], -1).reshape(-1)
    face = jnp.asarray(face_matrix(), BF)
    spread = jnp.asarray(spread_matrix(), BF)
    vm = pl.BlockSpec(memory_space=pltpu.VMEM)
    dma = pltpu.SemaphoreType.DMA
    out, ig, grads = pl.pallas_call(
        functools.partial(kernel, n_gx, n_gy, rz),
        out_shape=(jax.ShapeDtypeStruct((rows, C), BF), jax.ShapeDtypeStruct((rows, C), F32),
                   jax.ShapeDtypeStruct((2, taps, C), BF)),
        in_specs=[vm] * 8,
        out_specs=(vm, vm, vm),
        scratch_shapes=[
            pltpu.VMEM((2, GRID, 2 * C), BF),
            pltpu.VMEM((2, 256, 2 * C), BF),
            pltpu.VMEM((2, 2, PLANE, 2 * C), BF),
            pltpu.VMEM((2, 2, 160, 2 * C), BF),
            pltpu.VMEM((EXT, TAPS), BF),
            pltpu.VMEM((EXT, TAPS), BF),
            pltpu.VMEM((EXT, TAPS), BF),
            pltpu.VMEM((EXT, TAPS), BF),
            pltpu.VMEM((C, 3 * TAPS), BF),
            pltpu.VMEM((C, 3 * TAPS), BF),
            pltpu.VMEM((2, taps, C), F32),
            pltpu.VMEM((2, half, C), BF),
            pltpu.VMEM((2, half, C), BF),
            pltpu.VMEM((2, half, C), BF),
            pltpu.VMEM((2, np_ - 1, quarter, C), BF),
            pltpu.VMEM((2, pad, C), F32),
            pltpu.VMEM((2, pad, C), BF),
            pltpu.VMEM((2, n3 - 1, rz, C), BF),
            pltpu.VMEM((2, 2 * np_ * pad, C), BF),
            dma((2, 8)), dma((2, 8)),
            dma((2,)), dma((2,)),
            dma((2, np_ - 1)), dma((2, np_ - 1)),
            dma((2, n3 - 1)), dma((2, n3 - 1)),
            dma((2, n3 - 1)), dma((2, n3 - 1)),
            dma((2, np_ - 1)), dma((2, np_ - 1)),
            dma((2,)), dma((2,)),
        ],
        compiler_params=pltpu.CompilerParams(
            collective_id=0, has_side_effects=True, vmem_limit_bytes=56 * 1024 * 1024),
        cost_estimate=pl.CostEstimate(flops=5_000_000_000, bytes_accessed=8_000_000,
                                      transcendentals=200_000),
    )(features, cotangent, target.reshape(1, rows), target.reshape(rows, 1),
      weight_one, weight_two, face, spread)
    scale = 1.0 / np.sqrt(np.float32(rows * n_gx * n_gy))
    grad_two = grads[0].astype(F32) * scale
    grad_one = grads[1].astype(F32) * scale
    return out, ig, grad_one, grad_two


def solution(mesh):
    shape = dict(mesh.shape)
    in_specs = (P(("gx", "gy"), None), P(("gx", "gy"), None), P(("gx", "gy")), P(), P())
    out_specs = (P(("gx", "gy"), None), P(("gx", "gy"), None), P(), P())
    return jax.shard_map(
        functools.partial(per_device, shape["gx"], shape["gy"]),
        mesh=mesh, in_specs=in_specs, out_specs=out_specs, check_vma=False,
    )
```

```python
import functools

import jax
import jax.numpy as jnp
import numpy as np
from jax import lax
from jax.experimental import pallas as pl
from jax.experimental.pallas import tpu as pltpu
from jax.sharding import PartitionSpec as P

PLANE = 96
GRID = 768
EXT = 960
C = 128
TAPS = 9 * C
MESH = pl.DeviceIdType.MESH
BF = jnp.bfloat16
F32 = jnp.float32


def dot(a, b):
    return jnp.dot(a, b, preferred_element_type=F32)


def dot_nt(a, b):
    return lax.dot_general(a, b, (((1,), (1,)), ((), ())), preferred_element_type=F32)


def kernel(n_gx, n_gy, rz, pos, feat, cot, w1_any, w2_any,
           out_ref, ig_ref, grad_ref,
           gp, yf, xr, yr, fx, fu, fh, fg, w1, w2, wt1, wt2, spread, acc, send_c, recv_c, s1b,
           recv_p, s2f, s2b, recv_z, gat,
           w_s, ex_s, ex_r, c_s, c_r, p_s, p_r, z_s, z_r, az_s, az_r, ap_s, ap_r, ac_s, ac_r):
    i = lax.axis_index("gx")
    j = lax.axis_index("gy")
    n3 = n_gx // 2
    ny = n_gy // 2
    np_ = 2 * ny
    half = acc.shape[1] // 2
    quarter = half // np_
    pad = rz * n3
    slots = feat.shape[0]
    core = lax.rem(j, 2)
    xb = lax.rem(i, 2)
    yb = j // 2
    me_p = yb * 2 + xb
    k = i // 2

    def shift(di, dj):
        return (lax.rem(i + di + n_gx, n_gx), lax.rem(j + dj + n_gy, n_gy))

    def plane_peer(r):
        rx, ry = r % 2, r // 2
        px = lax.rem(xb + rx, 2)
        py = lax.rem(yb + ry, ny)
        return (k * 2 + px, py * 2 + core), py * 2 + px

    def z_peer(d):
        pk = lax.rem(k + d, n3)
        return (pk * 2 + xb, j), pk

    other = (i, yb * 2 + (1 - core))
    dirs = [(a, b) for a in (-1, 0, 1) for b in (-1, 0, 1) if (a, b) != (0, 0)]

    barrier = pltpu.get_barrier_semaphore()
    targets = [shift(a, b) for a, b in dirs] + [other]
    targets += [plane_peer(r)[0] for r in range(1, np_)]
    targets += [z_peer(d)[0] for d in range(1, n3)]
    for t in targets:
        pl.semaphore_signal(barrier, inc=1, device_id=t, device_id_type=MESH)
    load_one = pltpu.make_async_copy(w1_any, w1, w_s.at[0])
    load_two = pltpu.make_async_copy(w2_any, w2, w_s.at[1])
    load_one.start()
    load_two.start()

    def remote(src, dst, ss, rs, dev):
        c = pltpu.make_async_remote_copy(src_ref=src, dst_ref=dst, send_sem=ss, recv_sem=rs,
                                         device_id=dev, device_id_type=MESH)
        c.start()
        return c

    def rows_at(shape, dim):
        row = lax.broadcasted_iota(jnp.int32, shape, dim)
        slot = row // 64
        inner = (row // 16 % 4) * PLANE + (row % 4) * 8 + row // 4 % 4
        at = jnp.full(shape, -1, jnp.int32)
        for s in range(slots // 64):
            p = pos[s]
            corner = p // 6 * (4 * PLANE) + p % 3 * 32 + p // 3 % 2 * 4
            corner = jnp.where(p >= 0, corner, -4 * GRID)
            at = jnp.where(slot == s, corner + inner, at)
        return at

    def one_hot(hit):
        return jnp.where(hit, 1.0, 0.0).astype(BF)

    place = one_hot(lax.broadcasted_iota(jnp.int32, (GRID, slots), 0) == rows_at((1, slots), 1))
    f_row = lax.broadcasted_iota(jnp.int32, (256, 1), 0)
    f_at = f_row // 16 % 8 * PLANE + f_row % 16 * 8 + f_row // 128 * 7
    f_at = jnp.where(f_row % 16 < 12, f_at, -1)
    face = one_hot(lax.broadcasted_iota(jnp.int32, (256, GRID), 1) == f_at)

    def put(f, a):
        gp[f] = a.astype(BF)
        yf[f] = dot(face, gp[f]).astype(BF)

    def exchange(e):
        copies = []
        for n, (a, b) in enumerate(dirs):
            if b == 0:
                src = gp.at[e, pl.ds(0 if a < 0 else GRID - PLANE, PLANE)]
                dst = xr.at[e, 1 if a < 0 else 0]
            else:
                base = 0 if b < 0 else 128
                side = 1 if b < 0 else 0
                if a == 0:
                    src = yf.at[e, pl.ds(base, 128)]
                    dst = yr.at[e, side, pl.ds(16, 128)]
                else:
                    src = yf.at[e, pl.ds(base + (0 if a < 0 else 112), 16)]
                    dst = yr.at[e, side, pl.ds(144 if a < 0 else 0, 16)]
            copies.append(remote(src, dst, ex_s.at[e, n], ex_r.at[e, n], shift(a, b)))
        return copies

    one = jnp.float32(1.0)
    zero = jnp.float32(0.0)
    lo_x = jnp.where(i > 0, one, zero)
    hi_x = jnp.where(i < n_gx - 1, one, zero)
    lo_y = jnp.where(j > 0, one, zero)
    hi_y = jnp.where(j < n_gy - 1, one, zero)

    def build(dst, e, copies):
        for c in copies:
            c.wait_recv()
        row = lax.broadcasted_iota(jnp.int32, (160, C), 0)
        edge = jnp.where(row < 16, lo_x, jnp.where(row >= 144, hi_x, one))
        ylo = dot(spread[0], (yr[e, 0].astype(F32) * (edge * lo_y)).astype(BF))
        yhi = dot(spread[1], (yr[e, 1].astype(F32) * (edge * hi_y)).astype(BF))
        xlo = xr[e, 0].astype(F32) * lo_x
        xhi = xr[e, 1].astype(F32) * hi_x
        ext = jnp.concatenate([xlo, gp[e].astype(F32), xhi], axis=0)
        ypos = lax.rem(lax.broadcasted_iota(jnp.int32, (EXT, C), 0), 8)
        below = jnp.where(ypos == 0, ylo, pltpu.roll(ext, 1, 0))
        above = jnp.where(ypos == 7, yhi, pltpu.roll(ext, EXT - 1, 0))
        blank = jnp.zeros((10, 8, C), F32)
        for dy, v in enumerate((below, ext, above)):
            v = v.reshape(10, PLANE, C)
            forms = (jnp.concatenate([blank, v[:, :PLANE - 8]], axis=1), v,
                     jnp.concatenate([v[:, 8:], blank], axis=1))
            for dz, w in enumerate(forms):
                o = (3 * dy + dz) * C
                dst[:, o:o + C] = w.reshape(EXT, C).astype(BF)

    def conv(f9, w):
        total = None
        for dx in range(3):
            t = dot(f9[dx * PLANE:dx * PLANE + GRID, :], w[dx * TAPS:(dx + 1) * TAPS, :])
            total = t if total is None else total + t
        return total

    def conv_t(f9, wt):
        total = None
        for dx in range(3):
            t = dot_nt(f9[dx * PLANE:dx * PLANE + GRID, :], wt[:, dx * TAPS:(dx + 1) * TAPS])
            total = t if total is None else total + t
        return total

    def core_start(g, left, f9):
        dx = g % 3
        t = dot(left, f9[dx * PLANE:dx * PLANE + GRID, :])
        for q in range(9):
            acc[g, (8 - q) * C:(9 - q) * C, :] = t[:, q * C:(q + 1) * C]
        send_c[g] = acc[g, pl.ds(pl.multiple_of((1 - core) * half, 16), half), :].astype(BF)
        return [remote(send_c.at[g], recv_c.at[g], c_s.at[g], c_r.at[g], other)]

    def plane_start(g):
        own = acc[g, pl.ds(pl.multiple_of(core * half, 16), half), :] + recv_c[g].astype(F32)
        s1b[g] = own.astype(BF)
        acc[g, pl.ds(pl.multiple_of(core * half, 16), half), :] = own
        copies = []
        for r in range(1, np_):
            dev, pq = plane_peer(r)
            copies.append(remote(s1b.at[g, pl.ds(pl.multiple_of(pq * quarter, 16), quarter)],
                                 recv_p.at[g, r - 1], p_s.at[g, r - 1], p_r.at[g, r - 1], dev))
        return copies

    def z_start(g):
        at = pl.multiple_of(core * half + me_p * quarter, 16)
        own = acc[g, pl.ds(at, quarter), :]
        for r in range(np_ - 1):
            own = own + recv_p[g, r].astype(F32)
        if pad > quarter:
            own = jnp.concatenate([own, jnp.zeros((pad - quarter, C), F32)], axis=0)
        s2f[g] = own
        s2b[g] = own.astype(BF)
        copies = []
        for d in range(1, n3):
            dev, pk = z_peer(d)
            copies.append(remote(s2b.at[g, pl.ds(pl.multiple_of(pk * rz, 16), rz)],
                                 recv_z.at[g, d - 1], z_s.at[g, d - 1], z_r.at[g, d - 1], dev))
        return copies

    def gather_z(g):
        own = s2f[g, pl.ds(pl.multiple_of(k * rz, 16), rz), :]
        for d in range(n3 - 1):
            own = own + recv_z[g, d].astype(F32)
        at = pl.multiple_of(k * rz, 16)
        gat[g, core * np_ + me_p, pl.ds(at, rz), :] = own.astype(BF)
        block = gat.at[g, core * np_ + me_p, pl.ds(at, rz)]
        return [remote(block, block, az_s.at[g, d - 1], az_r.at[g, d - 1], z_peer(d)[0])
                for d in range(1, n3)]

    def gather_plane(g):
        block = gat.at[g, core * np_ + me_p, pl.ds(0, quarter)]
        return [remote(block, block, ap_s.at[g, r - 1], ap_r.at[g, r - 1], plane_peer(r)[0])
                for r in range(1, np_)]

    def gather_core(g):
        block = gat.at[g, pl.ds(core * np_, np_), pl.ds(0, quarter)]
        return [remote(block, block, ac_s.at[g], ac_r.at[g], other)]

    def finish(g):
        first = (18 - 9 * (g % 3)) * C
        for q in range(2 * np_):
            at = first + q * quarter
            grad_ref[g // 3, at:at + quarter, :] = gat[g, q, 0:quarter, :]
        return []

    stages = (None, plane_start, z_start, gather_z, gather_plane, gather_core, finish)
    flight = {}
    pending = []

    def advance(*steps):
        for stage, g in steps:
            for c in flight[g]:
                c.wait_recv()
            flight[g] = stages[stage](g)
            pending.extend(flight[g])

    def begin(g, left, f9):
        flight[g] = core_start(g, left, f9)
        pending.extend(flight[g])

    xg = dot(place, feat[...])
    put(0, xg)
    pl.semaphore_wait(barrier, len(targets))
    ex_x = exchange(0)
    ug = dot(place, cot[...])
    put(1, ug)
    ex_u = exchange(1)
    mask = dot(place, jnp.ones((slots, C), BF))
    s_col = lax.broadcasted_iota(jnp.int32, (1, 160), 1)
    s_at = jnp.where(s_col % 16 < 12, s_col // 16 * PLANE + s_col % 16 * 8, -8)
    s_row = lax.broadcasted_iota(jnp.int32, (EXT, 160), 0)
    spread[0] = one_hot(s_row == s_at)
    spread[1] = one_hot(s_row == s_at + 7)
    load_one.wait()
    load_two.wait()
    for o in range(27):
        lanes = slice(o * C, (o + 1) * C)
        rows = slice((26 - o) * C, (27 - o) * C)
        wt1[:, lanes] = w1[rows, :]
        wt2[:, lanes] = w2[rows, :]
    x_t = jnp.transpose(xg).astype(BF)
    build(fx, 0, ex_x)
    pre = conv(fx, w1)
    sig = jax.nn.sigmoid(pre)
    hidden = pre * sig * mask
    h_t = jnp.transpose(hidden).astype(BF)
    build(fu, 1, ex_u)
    back = conv_t(fu, wt2)
    hgrad = back * (sig * (1.0 + pre * (1.0 - sig))) * mask
    put(3, hgrad)
    ex_g = exchange(3)
    put(2, hidden)
    ex_h = exchange(2)
    for g in range(3):
        begin(g, h_t, fu)
    advance((1, 0))
    build(fg, 3, ex_g)
    advance((1, 1), (1, 2))
    for g in range(3, 6):
        begin(g, x_t, fg)
    advance((2, 0), (1, 3))
    build(fh, 2, ex_h)
    advance((2, 1), (1, 4), (1, 5), (2, 2))
    pre_two = conv(fh, w2)
    advance((3, 0))
    pick = one_hot(lax.broadcasted_iota(jnp.int32, (slots, GRID), 1) == rows_at((slots, 1), 0))
    og = (pre_two + gp[0].astype(F32)).astype(BF)
    out_ref[...] = dot(pick, og).astype(BF)
    advance((3, 1), (2, 3), (3, 2))
    ig = conv_t(fg, wt1) + gp[1].astype(F32)
    advance((4, 0), (2, 4))
    ig_hi = ig.astype(BF)
    ig_lo = (ig - ig_hi.astype(F32)).astype(BF)
    ig_ref[...] = dot(pick, ig_hi) + dot(pick, ig_lo)
    advance((2, 5), (3, 3), (4, 1), (3, 4), (4, 2), (3, 5), (5, 0), (4, 3), (5, 1), (4, 4),
            (5, 2), (4, 5), (6, 0), (5, 3), (6, 1), (5, 4), (6, 2), (5, 5), (6, 3), (6, 4), (6, 5))
    for c in ex_x + ex_u + ex_g + ex_h + pending:
        c.wait_send()


def finish_kernel(scale, grads, out, ig, out_ref, ig_ref, one_ref, two_ref):
    out_ref[...] = out[...]
    ig_ref[...] = ig[...]
    two_ref[...] = grads[0].astype(F32) * scale
    one_ref[...] = grads[1].astype(F32) * scale


def per_device(n_gx, n_gy, features, cotangent, block_pos, weight_one, weight_two):
    rows = features.shape[0]
    n3 = n_gx // 2
    np_ = n_gy
    taps = weight_one.shape[0]
    group = taps // 3
    half = group // 2
    quarter = half // np_
    rz = -(-quarter // (16 * n3)) * 16
    pad = rz * n3
    vm = pl.BlockSpec(memory_space=pltpu.VMEM)
    dma = pltpu.SemaphoreType.DMA
    out, ig, grads = pl.pallas_call(
        functools.partial(kernel, n_gx, n_gy, rz),
        out_shape=(jax.ShapeDtypeStruct((rows, C), BF), jax.ShapeDtypeStruct((rows, C), F32),
                   jax.ShapeDtypeStruct((2, taps, C), BF)),
        in_specs=[pl.BlockSpec(memory_space=pltpu.SMEM), vm, vm,
                  pl.BlockSpec(memory_space=pl.ANY), pl.BlockSpec(memory_space=pl.ANY)],
        out_specs=(vm, vm, vm),
        scratch_shapes=[
            pltpu.VMEM((4, GRID, C), BF),
            pltpu.VMEM((4, 256, C), BF),
            pltpu.VMEM((4, 2, PLANE, C), BF),
            pltpu.VMEM((4, 2, 160, C), BF),
            pltpu.VMEM((EXT, TAPS), BF),
            pltpu.VMEM((EXT, TAPS), BF),
            pltpu.VMEM((EXT, TAPS), BF),
            pltpu.VMEM((EXT, TAPS), BF),
            pltpu.VMEM((taps, C), BF),
            pltpu.VMEM((taps, C), BF),
            pltpu.VMEM((C, taps), BF),
            pltpu.VMEM((C, taps), BF),
            pltpu.VMEM((2, EXT, 160), BF),
            pltpu.VMEM((6, group, C), F32),
            pltpu.VMEM((6, half, C), BF),
            pltpu.VMEM((6, half, C), BF),
            pltpu.VMEM((6, half, C), BF),
            pltpu.VMEM((6, np_ - 1, quarter, C), BF),
            pltpu.VMEM((6, pad, C), F32),
            pltpu.VMEM((6, pad, C), BF),
            pltpu.VMEM((6, n3 - 1, rz, C), BF),
            pltpu.VMEM((6, 2 * np_, pad, C), BF),
            dma((2,)),
            dma((4, 8)), dma((4, 8)),
            dma((6,)), dma((6,)),
            dma((6, np_ - 1)), dma((6, np_ - 1)),
            dma((6, n3 - 1)), dma((6, n3 - 1)),
            dma((6, n3 - 1)), dma((6, n3 - 1)),
            dma((6, np_ - 1)), dma((6, np_ - 1)),
            dma((6,)), dma((6,)),
        ],
        compiler_params=pltpu.CompilerParams(
            collective_id=0, has_side_effects=True, vmem_limit_bytes=56 * 1024 * 1024),
        cost_estimate=pl.CostEstimate(flops=5_000_000_000, bytes_accessed=8_000_000,
                                      transcendentals=200_000),
    )(block_pos, features, cotangent, weight_one, weight_two)
    scale = float(1.0 / np.sqrt(np.float32(rows * n_gx * n_gy)))
    steps = 4
    cut = lambda n: pl.BlockSpec((n // steps, C), lambda s: (s, 0))
    return tuple(pl.pallas_call(
        functools.partial(finish_kernel, scale),
        grid=(steps,),
        out_shape=(jax.ShapeDtypeStruct((rows, C), BF), jax.ShapeDtypeStruct((rows, C), F32),
                   jax.ShapeDtypeStruct((taps, C), F32), jax.ShapeDtypeStruct((taps, C), F32)),
        in_specs=[pl.BlockSpec((2, taps // steps, C), lambda s: (0, s, 0)), cut(rows), cut(rows)],
        out_specs=(cut(rows), cut(rows), cut(taps), cut(taps)),
    )(grads, out, ig))


def solution(mesh):
    shape = dict(mesh.shape)
    in_specs = (P(("gx", "gy"), None), P(("gx", "gy"), None), P(("gx", "gy")), P(), P())
    out_specs = (P(("gx", "gy"), None), P(("gx", "gy"), None), P(), P())
    return jax.shard_map(
        functools.partial(per_device, shape["gx"], shape["gy"]),
        mesh=mesh, in_specs=in_specs, out_specs=out_specs, check_vma=False,
    )
```

```python
import functools

import jax
import jax.numpy as jnp
import numpy as np
from jax import lax
from jax.experimental import pallas as pl
from jax.experimental.pallas import tpu as pltpu
from jax.sharding import PartitionSpec as P

PLANE = 96
GRID = 768
EXT = 960
C = 128
TAPS = 9 * C
MESH = pl.DeviceIdType.MESH
BF = jnp.bfloat16
F32 = jnp.float32


def dot(a, b):
    return jnp.dot(a, b, preferred_element_type=F32)


def dot_nt(a, b):
    return lax.dot_general(a, b, (((1,), (1,)), ((), ())), preferred_element_type=F32)


def kernel(n_gx, n_gy, rz, pos, feat, cot, w1_any, w2_any,
           out_ref, ig_ref, grad_ref,
           gp, yf, xr, yr, fx, fu, fh, fg, w1, w2, wt1, wt2, spread, acc, send_c, recv_c, s1b,
           recv_p, s2f, s2b, recv_z, gat,
           w_s, ex_s, ex_r, c_s, c_r, p_s, p_r, z_s, z_r, az_s, az_r, ap_s, ap_r, ac_s, ac_r):
    i = lax.axis_index("gx")
    j = lax.axis_index("gy")
    n3 = n_gx // 2
    ny = n_gy // 2
    np_ = 2 * ny
    half = acc.shape[1] // 2
    quarter = half // np_
    pad = rz * n3
    slots = feat.shape[0]
    core = lax.rem(j, 2)
    xb = lax.rem(i, 2)
    yb = j // 2
    me_p = yb * 2 + xb
    k = i // 2

    def shift(di, dj):
        return (lax.rem(i + di + n_gx, n_gx), lax.rem(j + dj + n_gy, n_gy))

    def plane_peer(r):
        rx, ry = r % 2, r // 2
        px = lax.rem(xb + rx, 2)
        py = lax.rem(yb + ry, ny)
        return (k * 2 + px, py * 2 + core), py * 2 + px

    def z_peer(d):
        pk = lax.rem(k + d, n3)
        return (pk * 2 + xb, j), pk

    other = (i, yb * 2 + (1 - core))
    dirs = [(a, b) for a in (-1, 0, 1) for b in (-1, 0, 1) if (a, b) != (0, 0)]

    barrier = pltpu.get_barrier_semaphore()
    targets = [shift(a, b) for a, b in dirs] + [other]
    targets += [plane_peer(r)[0] for r in range(1, np_)]
    targets += [z_peer(d)[0] for d in range(1, n3)]
    for t in targets:
        pl.semaphore_signal(barrier, inc=1, device_id=t, device_id_type=MESH)
    load_one = pltpu.make_async_copy(w1_any, w1, w_s.at[0])
    load_two = pltpu.make_async_copy(w2_any, w2, w_s.at[1])
    load_one.start()
    load_two.start()

    def remote(src, dst, ss, rs, dev):
        c = pltpu.make_async_remote_copy(src_ref=src, dst_ref=dst, send_sem=ss, recv_sem=rs,
                                         device_id=dev, device_id_type=MESH)
        c.start()
        return c

    def rows_at(shape, dim):
        row = lax.broadcasted_iota(jnp.int32, shape, dim)
        slot = row // 64
        inner = (row // 16 % 4) * PLANE + (row % 4) * 8 + row // 4 % 4
        at = jnp.full(shape, -1, jnp.int32)
        for s in range(slots // 64):
            p = pos[s]
            corner = p // 6 * (4 * PLANE) + p % 3 * 32 + p // 3 % 2 * 4
            corner = jnp.where(p >= 0, corner, -4 * GRID)
            at = jnp.where(slot == s, corner + inner, at)
        return at

    def one_hot(hit):
        return jnp.where(hit, 1.0, 0.0).astype(BF)

    place = one_hot(lax.broadcasted_iota(jnp.int32, (GRID, slots), 0) == rows_at((1, slots), 1))
    f_row = lax.broadcasted_iota(jnp.int32, (256, 1), 0)
    f_at = f_row // 16 % 8 * PLANE + f_row % 16 * 8 + f_row // 128 * 7
    f_at = jnp.where(f_row % 16 < 12, f_at, -1)
    face = one_hot(lax.broadcasted_iota(jnp.int32, (256, GRID), 1) == f_at)

    def put(f, a):
        gp[f] = a.astype(BF)
        yf[f] = dot(face, gp[f]).astype(BF)

    def exchange(e):
        copies = []
        for n, (a, b) in enumerate(dirs):
            if b == 0:
                src = gp.at[e, pl.ds(0 if a < 0 else GRID - PLANE, PLANE)]
                dst = xr.at[e, 1 if a < 0 else 0]
            else:
                base = 0 if b < 0 else 128
                side = 1 if b < 0 else 0
                if a == 0:
                    src = yf.at[e, pl.ds(base, 128)]
                    dst = yr.at[e, side, pl.ds(16, 128)]
                else:
                    src = yf.at[e, pl.ds(base + (0 if a < 0 else 112), 16)]
                    dst = yr.at[e, side, pl.ds(144 if a < 0 else 0, 16)]
            copies.append(remote(src, dst, ex_s.at[e, n], ex_r.at[e, n], shift(a, b)))
        return copies

    one = jnp.float32(1.0)
    zero = jnp.float32(0.0)
    lo_x = jnp.where(i > 0, one, zero)
    hi_x = jnp.where(i < n_gx - 1, one, zero)
    lo_y = jnp.where(j > 0, one, zero)
    hi_y = jnp.where(j < n_gy - 1, one, zero)

    def build(dst, e, copies):
        for c in copies:
            c.wait_recv()
        row = lax.broadcasted_iota(jnp.int32, (160, C), 0)
        edge = jnp.where(row < 16, lo_x, jnp.where(row >= 144, hi_x, one))
        ylo = dot(spread[0], (yr[e, 0].astype(F32) * (edge * lo_y)).astype(BF))
        yhi = dot(spread[1], (yr[e, 1].astype(F32) * (edge * hi_y)).astype(BF))
        xlo = xr[e, 0].astype(F32) * lo_x
        xhi = xr[e, 1].astype(F32) * hi_x
        ext = jnp.concatenate([xlo, gp[e].astype(F32), xhi], axis=0)
        ypos = lax.rem(lax.broadcasted_iota(jnp.int32, (EXT, C), 0), 8)
        below = jnp.where(ypos == 0, ylo, pltpu.roll(ext, 1, 0))
        above = jnp.where(ypos == 7, yhi, pltpu.roll(ext, EXT - 1, 0))
        blank = jnp.zeros((10, 8, C), F32)
        for dy, v in enumerate((below, ext, above)):
            v = v.reshape(10, PLANE, C)
            forms = (jnp.concatenate([blank, v[:, :PLANE - 8]], axis=1), v,
                     jnp.concatenate([v[:, 8:], blank], axis=1))
            for dz, w in enumerate(forms):
                o = (3 * dy + dz) * C
                dst[:, o:o + C] = w.reshape(EXT, C).astype(BF)

    def conv(f9, w):
        total = None
        for dx in range(3):
            t = dot(f9[dx * PLANE:dx * PLANE + GRID, :], w[dx * TAPS:(dx + 1) * TAPS, :])
            total = t if total is None else total + t
        return total

    def conv_t(f9, wt):
        total = None
        for dx in range(3):
            t = dot_nt(f9[dx * PLANE:dx * PLANE + GRID, :], wt[:, dx * TAPS:(dx + 1) * TAPS])
            total = t if total is None else total + t
        return total

    def core_start(g, left, f9):
        dx = g % 3
        t = dot(left, f9[dx * PLANE:dx * PLANE + GRID, :])
        for q in range(9):
            at = (8 - q if g < 3 else q) * C
            acc[g, at:at + C, :] = t[:, q * C:(q + 1) * C]
        send_c[g] = acc[g, pl.ds(pl.multiple_of((1 - core) * half, 16), half), :].astype(BF)
        return [remote(send_c.at[g], recv_c.at[g], c_s.at[g], c_r.at[g], other)]

    def plane_start(g):
        own = acc[g, pl.ds(pl.multiple_of(core * half, 16), half), :] + recv_c[g].astype(F32)
        s1b[g] = own.astype(BF)
        acc[g, pl.ds(pl.multiple_of(core * half, 16), half), :] = own
        copies = []
        for r in range(1, np_):
            dev, pq = plane_peer(r)
            copies.append(remote(s1b.at[g, pl.ds(pl.multiple_of(pq * quarter, 16), quarter)],
                                 recv_p.at[g, r - 1], p_s.at[g, r - 1], p_r.at[g, r - 1], dev))
        return copies

    def z_start(g):
        at = pl.multiple_of(core * half + me_p * quarter, 16)
        own = acc[g, pl.ds(at, quarter), :]
        for r in range(np_ - 1):
            own = own + recv_p[g, r].astype(F32)
        if pad > quarter:
            own = jnp.concatenate([own, jnp.zeros((pad - quarter, C), F32)], axis=0)
        s2f[g] = own
        s2b[g] = own.astype(BF)
        copies = []
        for d in range(1, n3):
            dev, pk = z_peer(d)
            copies.append(remote(s2b.at[g, pl.ds(pl.multiple_of(pk * rz, 16), rz)],
                                 recv_z.at[g, d - 1], z_s.at[g, d - 1], z_r.at[g, d - 1], dev))
        return copies

    def gather_z(g):
        own = s2f[g, pl.ds(pl.multiple_of(k * rz, 16), rz), :]
        for d in range(n3 - 1):
            own = own + recv_z[g, d].astype(F32)
        at = pl.multiple_of(k * rz, 16)
        gat[g, core * np_ + me_p, pl.ds(at, rz), :] = own.astype(BF)
        block = gat.at[g, core * np_ + me_p, pl.ds(at, rz)]
        return [remote(block, block, az_s.at[g, d - 1], az_r.at[g, d - 1], z_peer(d)[0])
                for d in range(1, n3)]

    def gather_plane(g):
        block = gat.at[g, core * np_ + me_p, pl.ds(0, quarter)]
        return [remote(block, block, ap_s.at[g, r - 1], ap_r.at[g, r - 1], plane_peer(r)[0])
                for r in range(1, np_)]

    def gather_core(g):
        block = gat.at[g, pl.ds(core * np_, np_), pl.ds(0, quarter)]
        return [remote(block, block, ac_s.at[g], ac_r.at[g], other)]

    def finish(g):
        if g < 3:
            first = (18 - 9 * g) * C
            for q in range(2 * np_):
                at = first + q * quarter
                grad_ref[0, at:at + quarter, :] = gat[g, q, 0:quarter, :]
        else:
            first = 9 * (g - 3) * C
            whole = jnp.concatenate([gat[g, q, 0:quarter, :] for q in range(2 * np_)], axis=0)
            for q in range(9):
                block = jnp.transpose(whole[q * C:(q + 1) * C, :].astype(F32))
                grad_ref[1, first + q * C:first + (q + 1) * C, :] = block.astype(BF)
        return []

    stages = (None, plane_start, z_start, gather_z, gather_plane, gather_core, finish)
    flight = {}
    pending = []

    def advance(*steps):
        for stage, g in steps:
            for c in flight[g]:
                c.wait_recv()
            flight[g] = stages[stage](g)
            pending.extend(flight[g])

    def begin(g, left, f9):
        flight[g] = core_start(g, left, f9)
        pending.extend(flight[g])

    xg = dot(place, feat[...])
    put(0, xg)
    pl.semaphore_wait(barrier, len(targets))
    ex_x = exchange(0)
    ug = dot(place, cot[...])
    put(1, ug)
    ex_u = exchange(1)
    mask = dot(place, jnp.ones((slots, C), BF))
    s_col = lax.broadcasted_iota(jnp.int32, (1, 160), 1)
    s_at = jnp.where(s_col % 16 < 12, s_col // 16 * PLANE + s_col % 16 * 8, -8)
    s_row = lax.broadcasted_iota(jnp.int32, (EXT, 160), 0)
    spread[0] = one_hot(s_row == s_at)
    spread[1] = one_hot(s_row == s_at + 7)
    load_one.wait()
    load_two.wait()
    for o in range(27):
        lanes = slice(o * C, (o + 1) * C)
        rows = slice((26 - o) * C, (27 - o) * C)
        wt1[:, lanes] = w1[rows, :]
        wt2[:, lanes] = w2[rows, :]
    build(fx, 0, ex_x)
    pre = conv(fx, w1)
    sig = jax.nn.sigmoid(pre)
    hidden = pre * sig * mask
    h_t = jnp.transpose(hidden).astype(BF)
    build(fu, 1, ex_u)
    for g in range(3):
        begin(g, h_t, fu)
    put(2, hidden)
    advance((1, 0))
    back = conv_t(fu, wt2)
    hgrad = back * (sig * (1.0 + pre * (1.0 - sig))) * mask
    hg_t = jnp.transpose(hgrad).astype(BF)
    advance((1, 1), (1, 2))
    for g in range(3, 6):
        begin(g, hg_t, fx)
    put(3, hgrad)
    ex_h = exchange(2)
    advance((1, 3))
    ex_g = exchange(3)
    advance((2, 0), (1, 4), (1, 5), (2, 1))
    build(fh, 2, ex_h)
    advance((2, 2), (3, 0))
    pre_two = conv(fh, w2)
    advance((3, 1), (2, 3))
    pick = one_hot(lax.broadcasted_iota(jnp.int32, (slots, GRID), 1) == rows_at((slots, 1), 0))
    og = (pre_two + gp[0].astype(F32)).astype(BF)
    out_ref[...] = dot(pick, og).astype(BF)
    advance((3, 2), (4, 0), (2, 4))
    build(fg, 3, ex_g)
    advance((4, 1), (2, 5), (3, 3))
    ig = conv_t(fg, wt1) + gp[1].astype(F32)
    advance((4, 2), (3, 4), (5, 0), (3, 5))
    ig_hi = ig.astype(BF)
    ig_lo = (ig - ig_hi.astype(F32)).astype(BF)
    ig_ref[...] = dot(pick, ig_hi) + dot(pick, ig_lo)
    advance((4, 3), (5, 1), (4, 4), (5, 2), (4, 5), (6, 0), (6, 1), (6, 2), (5, 3), (5, 4), (5, 5),
            (6, 3), (6, 4), (6, 5))
    for c in ex_x + ex_u + ex_g + ex_h + pending:
        c.wait_send()


def finish_kernel(scale, parts, grads, out, ig, out_ref, ig_ref, one_ref, two_ref,
                  narrow, wide, in_s, out_s, side_s):
    size = grads.shape[1] // parts
    chunks = [(g, q) for q in range(parts) for g in range(2)]
    loads = []
    for n, (g, q) in enumerate(chunks):
        loads.append(pltpu.make_async_copy(
            grads.at[g, pl.ds(q * size, size)], narrow.at[n], in_s.at[n]))
        loads[-1].start()
    ends = [pltpu.make_async_copy(out, out_ref, side_s.at[0]),
            pltpu.make_async_copy(ig, ig_ref, side_s.at[1])]
    for c in ends:
        c.start()
    for n, (g, q) in enumerate(chunks):
        loads[n].wait()
        wide[n] = narrow[n].astype(F32) * scale
        to = one_ref if g else two_ref
        ends.append(pltpu.make_async_copy(wide.at[n], to.at[pl.ds(q * size, size)], out_s.at[n]))
        ends[-1].start()
    for c in ends:
        c.wait()


def per_device(n_gx, n_gy, features, cotangent, block_pos, weight_one, weight_two):
    rows = features.shape[0]
    n3 = n_gx // 2
    np_ = n_gy
    taps = weight_one.shape[0]
    group = taps // 3
    half = group // 2
    quarter = half // np_
    rz = -(-quarter // (16 * n3)) * 16
    pad = rz * n3
    vm = pl.BlockSpec(memory_space=pltpu.VMEM)
    dma = pltpu.SemaphoreType.DMA
    out, ig, grads = pl.pallas_call(
        functools.partial(kernel, n_gx, n_gy, rz),
        out_shape=(jax.ShapeDtypeStruct((rows, C), BF), jax.ShapeDtypeStruct((rows, C), F32),
                   jax.ShapeDtypeStruct((2, taps, C), BF)),
        in_specs=[pl.BlockSpec(memory_space=pltpu.SMEM), vm, vm,
                  pl.BlockSpec(memory_space=pl.ANY), pl.BlockSpec(memory_space=pl.ANY)],
        out_specs=(vm, vm, vm),
        scratch_shapes=[
            pltpu.VMEM((4, GRID, C), BF),
            pltpu.VMEM((4, 256, C), BF),
            pltpu.VMEM((4, 2, PLANE, C), BF),
            pltpu.VMEM((4, 2, 160, C), BF),
            pltpu.VMEM((EXT, TAPS), BF),
            pltpu.VMEM((EXT, TAPS), BF),
            pltpu.VMEM((EXT, TAPS), BF),
            pltpu.VMEM((EXT, TAPS), BF),
            pltpu.VMEM((taps, C), BF),
            pltpu.VMEM((taps, C), BF),
            pltpu.VMEM((C, taps), BF),
            pltpu.VMEM((C, taps), BF),
            pltpu.VMEM((2, EXT, 160), BF),
            pltpu.VMEM((6, group, C), F32),
            pltpu.VMEM((6, half, C), BF),
            pltpu.VMEM((6, half, C), BF),
            pltpu.VMEM((6, half, C), BF),
            pltpu.VMEM((6, np_ - 1, quarter, C), BF),
            pltpu.VMEM((6, pad, C), F32),
            pltpu.VMEM((6, pad, C), BF),
            pltpu.VMEM((6, n3 - 1, rz, C), BF),
            pltpu.VMEM((6, 2 * np_, pad, C), BF),
            dma((2,)),
            dma((4, 8)), dma((4, 8)),
            dma((6,)), dma((6,)),
            dma((6, np_ - 1)), dma((6, np_ - 1)),
            dma((6, n3 - 1)), dma((6, n3 - 1)),
            dma((6, n3 - 1)), dma((6, n3 - 1)),
            dma((6, np_ - 1)), dma((6, np_ - 1)),
            dma((6,)), dma((6,)),
        ],
        compiler_params=pltpu.CompilerParams(
            collective_id=0, has_side_effects=True, vmem_limit_bytes=56 * 1024 * 1024),
        cost_estimate=pl.CostEstimate(flops=5_000_000_000, bytes_accessed=8_000_000,
                                      transcendentals=200_000),
    )(block_pos, features, cotangent, weight_one, weight_two)
    scale = float(1.0 / np.sqrt(np.float32(rows * n_gx * n_gy)))
    parts = 6
    hbm = pl.BlockSpec(memory_space=pl.ANY)
    return tuple(pl.pallas_call(
        functools.partial(finish_kernel, scale, parts),
        out_shape=(jax.ShapeDtypeStruct((rows, C), BF), jax.ShapeDtypeStruct((rows, C), F32),
                   jax.ShapeDtypeStruct((taps, C), F32), jax.ShapeDtypeStruct((taps, C), F32)),
        in_specs=[hbm] * 3,
        out_specs=(hbm,) * 4,
        scratch_shapes=[
            pltpu.VMEM((2 * parts, taps // parts, C), BF),
            pltpu.VMEM((2 * parts, taps // parts, C), F32),
            dma((2 * parts,)), dma((2 * parts,)), dma((2,)),
        ],
        compiler_params=pltpu.CompilerParams(vmem_limit_bytes=56 * 1024 * 1024),
    )(grads, out, ig))


def solution(mesh):
    shape = dict(mesh.shape)
    in_specs = (P(("gx", "gy"), None), P(("gx", "gy"), None), P(("gx", "gy")), P(), P())
    out_specs = (P(("gx", "gy"), None), P(("gx", "gy"), None), P(), P())
    return jax.shard_map(
        functools.partial(per_device, shape["gx"], shape["gy"]),
        mesh=mesh, in_specs=in_specs, out_specs=out_specs, check_vma=False,
    )
```

```python
import functools

import jax
import jax.numpy as jnp
import numpy as np
from jax import lax
from jax.experimental import pallas as pl
from jax.experimental.pallas import tpu as pltpu
from jax.sharding import PartitionSpec as P

PLANE = 96
GRID = 768
EXT = 960
C = 128
TAPS = 9 * C
MESH = pl.DeviceIdType.MESH
BF = jnp.bfloat16
F32 = jnp.float32


def dot(a, b):
    return jnp.dot(a, b, preferred_element_type=F32)


def dot_nt(a, b):
    return lax.dot_general(a, b, (((1,), (1,)), ((), ())), preferred_element_type=F32)


def kernel(n_gx, n_gy, rz, pos, feat, cot, w1_any, w2_any,
           out_ref, ig_ref, grad_ref,
           gp, yf, xr, yr, fx, fu, fh, fg, w1, w2, wt1, wt2, spread, acc, send_c, recv_c, s1b,
           recv_p, s2f, s2b, recv_z, gat,
           w_s, ex_s, ex_r, c_s, c_r, p_s, p_r, z_s, z_r, az_s, az_r, ap_s, ap_r, ac_s, ac_r):
    i = lax.axis_index("gx")
    j = lax.axis_index("gy")
    n3 = n_gx // 2
    ny = n_gy // 2
    np_ = 2 * ny
    half = acc.shape[1] // 2
    quarter = half // np_
    pad = rz * n3
    slots = feat.shape[0]
    core = lax.rem(j, 2)
    xb = lax.rem(i, 2)
    yb = j // 2
    me_p = yb * 2 + xb
    k = i // 2

    def shift(di, dj):
        return (lax.rem(i + di + n_gx, n_gx), lax.rem(j + dj + n_gy, n_gy))

    def plane_peer(r):
        rx, ry = r % 2, r // 2
        px = lax.rem(xb + rx, 2)
        py = lax.rem(yb + ry, ny)
        return (k * 2 + px, py * 2 + core), py * 2 + px

    def z_peer(d):
        pk = lax.rem(k + d, n3)
        return (pk * 2 + xb, j), pk

    other = (i, yb * 2 + (1 - core))
    dirs = [(a, b) for a in (-1, 0, 1) for b in (-1, 0, 1) if (a, b) != (0, 0)]

    barrier = pltpu.get_barrier_semaphore()
    targets = [shift(a, b) for a, b in dirs] + [other]
    targets += [plane_peer(r)[0] for r in range(1, np_)]
    targets += [z_peer(d)[0] for d in range(1, n3)]
    for t in targets:
        pl.semaphore_signal(barrier, inc=1, device_id=t, device_id_type=MESH)
    load_one = pltpu.make_async_copy(w1_any, w1, w_s.at[0])
    load_two = pltpu.make_async_copy(w2_any, w2, w_s.at[1])
    load_one.start()
    load_two.start()

    def remote(src, dst, ss, rs, dev):
        c = pltpu.make_async_remote_copy(src_ref=src, dst_ref=dst, send_sem=ss, recv_sem=rs,
                                         device_id=dev, device_id_type=MESH)
        c.start()
        return c

    def rows_at(shape, dim):
        row = lax.broadcasted_iota(jnp.int32, shape, dim)
        slot = row >> 6
        inner = ((row >> 4) & 3) * PLANE + (row & 3) * 8 + ((row >> 2) & 3)
        at = jnp.full(shape, -1, jnp.int32)
        for s in range(slots // 64):
            p = pos[s]
            third = (p * 86) >> 8
            corner = (third >> 1) * (4 * PLANE) + (p - 3 * third) * 32 + (third & 1) * 4
            corner = jnp.where(p >= 0, corner, -4 * GRID)
            at = jnp.where(slot == s, corner + inner, at)
        return at

    def one_hot(hit):
        return jnp.where(hit, 1.0, 0.0).astype(BF)

    place = one_hot(lax.broadcasted_iota(jnp.int32, (GRID, slots), 0) == rows_at((1, slots), 1))
    f_row = lax.broadcasted_iota(jnp.int32, (256, 1), 0)
    f_at = ((f_row >> 4) & 7) * PLANE + (f_row & 15) * 8 + (f_row >> 7) * 7
    f_at = jnp.where((f_row & 15) < 12, f_at, -1)
    face = one_hot(lax.broadcasted_iota(jnp.int32, (256, GRID), 1) == f_at)

    def put(f, a):
        gp[f] = a.astype(BF)
        yf[f] = dot(face, gp[f]).astype(BF)

    def exchange(e, first, count):
        fields = pl.ds(first, count)
        copies = []
        for n, (a, b) in enumerate(dirs):
            if b == 0:
                src = gp.at[fields, pl.ds(0 if a < 0 else GRID - PLANE, PLANE)]
                dst = xr.at[fields, 1 if a < 0 else 0]
            else:
                base = 0 if b < 0 else 128
                side = 1 if b < 0 else 0
                if a == 0:
                    src = yf.at[fields, pl.ds(base, 128)]
                    dst = yr.at[fields, side, pl.ds(16, 128)]
                else:
                    src = yf.at[fields, pl.ds(base + (0 if a < 0 else 112), 16)]
                    dst = yr.at[fields, side, pl.ds(144 if a < 0 else 0, 16)]
            copies.append(remote(src, dst, ex_s.at[e, n], ex_r.at[e, n], shift(a, b)))
        return copies

    one = jnp.float32(1.0)
    zero = jnp.float32(0.0)
    lo_x = jnp.where(i > 0, one, zero)
    hi_x = jnp.where(i < n_gx - 1, one, zero)
    lo_y = jnp.where(j > 0, one, zero)
    hi_y = jnp.where(j < n_gy - 1, one, zero)

    def build(dst, e):
        row = lax.broadcasted_iota(jnp.int32, (160, C), 0)
        edge = jnp.where(row < 16, lo_x, jnp.where(row >= 144, hi_x, one))
        ylo = dot(spread[0], (yr[e, 0].astype(F32) * (edge * lo_y)).astype(BF))
        yhi = dot(spread[1], (yr[e, 1].astype(F32) * (edge * hi_y)).astype(BF))
        xlo = xr[e, 0].astype(F32) * lo_x
        xhi = xr[e, 1].astype(F32) * hi_x
        ext = jnp.concatenate([xlo, gp[e].astype(F32), xhi], axis=0)
        ypos = lax.broadcasted_iota(jnp.int32, (EXT, C), 0) & 7
        below = jnp.where(ypos == 0, ylo, pltpu.roll(ext, 1, 0))
        above = jnp.where(ypos == 7, yhi, pltpu.roll(ext, EXT - 1, 0))
        blank = jnp.zeros((10, 8, C), F32)
        for dy, v in enumerate((below, ext, above)):
            v = v.reshape(10, PLANE, C)
            forms = (jnp.concatenate([blank, v[:, :PLANE - 8]], axis=1), v,
                     jnp.concatenate([v[:, 8:], blank], axis=1))
            for dz, w in enumerate(forms):
                o = (3 * dy + dz) * C
                dst[:, o:o + C] = w.reshape(EXT, C).astype(BF)

    def conv(f9, w):
        total = None
        for dx in range(3):
            t = dot(f9[dx * PLANE:dx * PLANE + GRID, :], w[dx * TAPS:(dx + 1) * TAPS, :])
            total = t if total is None else total + t
        return total

    def conv_t(f9, wt):
        total = None
        for dx in range(3):
            t = dot_nt(f9[dx * PLANE:dx * PLANE + GRID, :], wt[:, dx * TAPS:(dx + 1) * TAPS])
            total = t if total is None else total + t
        return total

    def core_start(g, lefts, f9s):
        for m in range(2):
            n = 2 * g + m
            dx = n % 3
            t = dot(lefts[m], f9s[m][dx * PLANE:dx * PLANE + GRID, :])
            for q in range(9):
                at = m * TAPS + (8 - q if n < 3 else q) * C
                acc[g, at:at + C, :] = t[:, q * C:(q + 1) * C]
        send_c[g] = acc[g, pl.ds(pl.multiple_of((1 - core) * half, 16), half), :].astype(BF)
        return [remote(send_c.at[g], recv_c.at[g], c_s.at[g], c_r.at[g], other)]

    def plane_start(g):
        own = acc[g, pl.ds(pl.multiple_of(core * half, 16), half), :] + recv_c[g].astype(F32)
        s1b[g] = own.astype(BF)
        acc[g, pl.ds(pl.multiple_of(core * half, 16), half), :] = own
        copies = []
        for r in range(1, np_):
            dev, pq = plane_peer(r)
            copies.append(remote(s1b.at[g, pl.ds(pl.multiple_of(pq * quarter, 16), quarter)],
                                 recv_p.at[g, r - 1], p_s.at[g, r - 1], p_r.at[g, r - 1], dev))
        return copies

    def z_start(g):
        at = pl.multiple_of(core * half + me_p * quarter, 16)
        own = acc[g, pl.ds(at, quarter), :]
        for r in range(np_ - 1):
            own = own + recv_p[g, r].astype(F32)
        if pad > quarter:
            own = jnp.concatenate([own, jnp.zeros((pad - quarter, C), F32)], axis=0)
        s2f[g] = own
        s2b[g] = own.astype(BF)
        copies = []
        for d in range(1, n3):
            dev, pk = z_peer(d)
            copies.append(remote(s2b.at[g, pl.ds(pl.multiple_of(pk * rz, 16), rz)],
                                 recv_z.at[g, d - 1], z_s.at[g, d - 1], z_r.at[g, d - 1], dev))
        return copies

    def gather_z(g):
        own = s2f[g, pl.ds(pl.multiple_of(k * rz, 16), rz), :]
        for d in range(n3 - 1):
            own = own + recv_z[g, d].astype(F32)
        at = pl.multiple_of(k * rz, 16)
        gat[g, core * np_ + me_p, pl.ds(at, rz), :] = own.astype(BF)
        block = gat.at[g, core * np_ + me_p, pl.ds(at, rz)]
        return [remote(block, block, az_s.at[g, d - 1], az_r.at[g, d - 1], z_peer(d)[0])
                for d in range(1, n3)]

    def gather_plane(g):
        block = gat.at[g, core * np_ + me_p, pl.ds(0, quarter)]
        return [remote(block, block, ap_s.at[g, r - 1], ap_r.at[g, r - 1], plane_peer(r)[0])
                for r in range(1, np_)]

    def gather_core(g):
        block = gat.at[g, pl.ds(core * np_, np_), pl.ds(0, quarter)]
        return [remote(block, block, ac_s.at[g], ac_r.at[g], other)]

    def finish(g):
        for m in range(2):
            n = 2 * g + m
            parts = [gat[g, m * np_ + q, 0:quarter, :] for q in range(np_)]
            if n < 3:
                for q in range(np_):
                    at = (18 - 9 * n) * C + q * quarter
                    grad_ref[0, at:at + quarter, :] = parts[q]
            else:
                whole = jnp.concatenate(parts, axis=0)
                for q in range(9):
                    at = (9 * (n - 3) + q) * C
                    block = jnp.transpose(whole[q * C:(q + 1) * C, :].astype(F32))
                    grad_ref[1, at:at + C, :] = block.astype(BF)
        return []

    stages = (None, plane_start, z_start, gather_z, gather_plane, gather_core, finish)
    flight = {}
    pending = []

    def advance(*steps):
        for stage, g in steps:
            for c in flight[g]:
                c.wait_recv()
            flight[g] = stages[stage](g)
            pending.extend(flight[g])

    def begin(g, lefts, f9s):
        flight[g] = core_start(g, lefts, f9s)
        pending.extend(flight[g])

    def landed(copies):
        for c in copies:
            c.wait_recv()

    xg = dot(place, feat[...])
    put(0, xg)
    pl.semaphore_wait(barrier, len(targets))
    ex_x = exchange(0, 0, 1)
    ug = dot(place, cot[...])
    put(1, ug)
    ex_u = exchange(1, 1, 1)
    mask = dot(place, jnp.ones((slots, C), BF))
    s_col = lax.broadcasted_iota(jnp.int32, (1, 160), 1)
    s_at = jnp.where((s_col & 15) < 12, (s_col >> 4) * PLANE + (s_col & 15) * 8, -8)
    s_row = lax.broadcasted_iota(jnp.int32, (EXT, 160), 0)
    spread[0] = one_hot(s_row == s_at)
    spread[1] = one_hot(s_row == s_at + 7)
    load_one.wait()
    load_two.wait()
    for o in range(27):
        lanes = slice(o * C, (o + 1) * C)
        rows = slice((26 - o) * C, (27 - o) * C)
        wt1[:, lanes] = w1[rows, :]
        wt2[:, lanes] = w2[rows, :]
    landed(ex_x)
    build(fx, 0)
    pre = conv(fx, w1)
    sig = jax.nn.sigmoid(pre)
    hidden = pre * sig * mask
    h_t = jnp.transpose(hidden).astype(BF)
    landed(ex_u)
    build(fu, 1)
    begin(0, (h_t, h_t), (fu, fu))
    put(2, hidden)
    back = conv_t(fu, wt2)
    hgrad = back * (sig * (1.0 + pre * (1.0 - sig))) * mask
    advance((1, 0))
    hg_t = jnp.transpose(hgrad).astype(BF)
    begin(1, (h_t, hg_t), (fu, fx))
    begin(2, (hg_t, hg_t), (fx, fx))
    advance((1, 1))
    put(3, hgrad)
    ex_h = exchange(2, 2, 2)
    advance((2, 0), (1, 2))
    landed(ex_h)
    build(fh, 2)
    advance((3, 0), (2, 1))
    pre_two = conv(fh, w2)
    pick = one_hot(lax.broadcasted_iota(jnp.int32, (slots, GRID), 1) == rows_at((slots, 1), 0))
    advance((4, 0))
    og = (pre_two + gp[0].astype(F32)).astype(BF)
    out_ref[...] = dot(pick, og).astype(BF)
    advance((3, 1), (2, 2))
    build(fg, 3)
    advance((4, 1))
    ig = conv_t(fg, wt1) + gp[1].astype(F32)
    advance((5, 0), (3, 2))
    ig_hi = ig.astype(BF)
    ig_lo = (ig - ig_hi.astype(F32)).astype(BF)
    ig_ref[...] = dot(pick, ig_hi) + dot(pick, ig_lo)
    advance((4, 2), (6, 0), (5, 1), (6, 1), (5, 2), (6, 2))
    for c in ex_x + ex_u + ex_h + pending:
        c.wait_send()


def finish_kernel(scale, parts, grads, out, ig, out_ref, ig_ref, one_ref, two_ref,
                  narrow, wide, side_out, side_ig, in_s, out_s, side_s):
    size = grads.shape[1] // parts
    chunks = [(g, q) for q in range(parts) for g in range(2)]
    loads = []
    for n, (g, q) in enumerate(chunks):
        loads.append(pltpu.make_async_copy(
            grads.at[g, pl.ds(q * size, size)], narrow.at[n], in_s.at[n]))
        loads[-1].start()
    sides = [pltpu.make_async_copy(out, side_out, side_s.at[0]),
             pltpu.make_async_copy(ig, side_ig, side_s.at[1])]
    for c in sides:
        c.start()
    ends = []
    for n, (g, q) in enumerate(chunks):
        loads[n].wait()
        wide[n] = narrow[n].astype(F32) * scale
        to = one_ref if g else two_ref
        ends.append(pltpu.make_async_copy(wide.at[n], to.at[pl.ds(q * size, size)], out_s.at[n]))
        ends[-1].start()
    backs = [pltpu.make_async_copy(side_out, out_ref, side_s.at[2]),
             pltpu.make_async_copy(side_ig, ig_ref, side_s.at[3])]
    for a, b in zip(sides, backs):
        a.wait()
        b.start()
    for c in ends + backs:
        c.wait()


def per_device(n_gx, n_gy, features, cotangent, block_pos, weight_one, weight_two):
    rows = features.shape[0]
    n3 = n_gx // 2
    np_ = n_gy
    taps = weight_one.shape[0]
    group = 2 * taps // 3
    half = group // 2
    quarter = half // np_
    rz = -(-quarter // (16 * n3)) * 16
    pad = rz * n3
    vm = pl.BlockSpec(memory_space=pltpu.VMEM)
    dma = pltpu.SemaphoreType.DMA
    out, ig, grads = pl.pallas_call(
        functools.partial(kernel, n_gx, n_gy, rz),
        out_shape=(jax.ShapeDtypeStruct((rows, C), BF), jax.ShapeDtypeStruct((rows, C), F32),
                   jax.ShapeDtypeStruct((2, taps, C), BF)),
        in_specs=[pl.BlockSpec(memory_space=pltpu.SMEM), vm, vm,
                  pl.BlockSpec(memory_space=pl.ANY), pl.BlockSpec(memory_space=pl.ANY)],
        out_specs=(vm, vm, vm),
        scratch_shapes=[
            pltpu.VMEM((4, GRID, C), BF),
            pltpu.VMEM((4, 256, C), BF),
            pltpu.VMEM((4, 2, PLANE, C), BF),
            pltpu.VMEM((4, 2, 160, C), BF),
            pltpu.VMEM((EXT, TAPS), BF),
            pltpu.VMEM((EXT, TAPS), BF),
            pltpu.VMEM((EXT, TAPS), BF),
            pltpu.VMEM((EXT, TAPS), BF),
            pltpu.VMEM((taps, C), BF),
            pltpu.VMEM((taps, C), BF),
            pltpu.VMEM((C, taps), BF),
            pltpu.VMEM((C, taps), BF),
            pltpu.VMEM((2, EXT, 160), BF),
            pltpu.VMEM((3, group, C), F32),
            pltpu.VMEM((3, half, C), BF),
            pltpu.VMEM((3, half, C), BF),
            pltpu.VMEM((3, half, C), BF),
            pltpu.VMEM((3, np_ - 1, quarter, C), BF),
            pltpu.VMEM((3, pad, C), F32),
            pltpu.VMEM((3, pad, C), BF),
            pltpu.VMEM((3, n3 - 1, rz, C), BF),
            pltpu.VMEM((3, 2 * np_, pad, C), BF),
            dma((2,)),
            dma((3, 8)), dma((3, 8)),
            dma((3,)), dma((3,)),
            dma((3, np_ - 1)), dma((3, np_ - 1)),
            dma((3, n3 - 1)), dma((3, n3 - 1)),
            dma((3, n3 - 1)), dma((3, n3 - 1)),
            dma((3, np_ - 1)), dma((3, np_ - 1)),
            dma((3,)), dma((3,)),
        ],
        compiler_params=pltpu.CompilerParams(
            collective_id=0, has_side_effects=True, vmem_limit_bytes=56 * 1024 * 1024),
        cost_estimate=pl.CostEstimate(flops=5_000_000_000, bytes_accessed=8_000_000,
                                      transcendentals=200_000),
    )(block_pos, features, cotangent, weight_one, weight_two)
    scale = float(1.0 / np.sqrt(np.float32(rows * n_gx * n_gy)))
    parts = 6
    hbm = pl.BlockSpec(memory_space=pl.ANY)
    return tuple(pl.pallas_call(
        functools.partial(finish_kernel, scale, parts),
        out_shape=(jax.ShapeDtypeStruct((rows, C), BF), jax.ShapeDtypeStruct((rows, C), F32),
                   jax.ShapeDtypeStruct((taps, C), F32), jax.ShapeDtypeStruct((taps, C), F32)),
        in_specs=[hbm] * 3,
        out_specs=(hbm,) * 4,
        scratch_shapes=[
            pltpu.VMEM((2 * parts, taps // parts, C), BF),
            pltpu.VMEM((2 * parts, taps // parts, C), F32),
            pltpu.VMEM((rows, C), BF), pltpu.VMEM((rows, C), F32),
            dma((2 * parts,)), dma((2 * parts,)), dma((4,)),
        ],
        compiler_params=pltpu.CompilerParams(vmem_limit_bytes=56 * 1024 * 1024),
    )(grads, out, ig))


def solution(mesh):
    shape = dict(mesh.shape)
    in_specs = (P(("gx", "gy"), None), P(("gx", "gy"), None), P(("gx", "gy")), P(), P())
    out_specs = (P(("gx", "gy"), None), P(("gx", "gy"), None), P(), P())
    return jax.shard_map(
        functools.partial(per_device, shape["gx"], shape["gy"]),
        mesh=mesh, in_specs=in_specs, out_specs=out_specs, check_vma=False,
    )
```

```python
import functools

import jax
import jax.numpy as jnp
import numpy as np
from jax import lax
from jax.experimental import pallas as pl
from jax.experimental.pallas import tpu as pltpu
from jax.sharding import PartitionSpec as P

PLANE = 96
GRID = 768
EXT = 960
C = 128
TAPS = 9 * C
MESH = pl.DeviceIdType.MESH
BF = jnp.bfloat16
F32 = jnp.float32


def dot(a, b):
    return jnp.dot(a, b, preferred_element_type=F32)


def dot_nt(a, b):
    return lax.dot_general(a, b, (((1,), (1,)), ((), ())), preferred_element_type=F32)


def kernel(n_gx, n_gy, rz, pos, feat, cot, w1_any, w2_any,
           out_ref, ig_ref, grad_ref,
           gp, yf, xr, yr, fx, fu, fh, fg, w1, w2, wt1, wt2, spread, acc, send_c, recv_c, s1b,
           recv_p, s2f, s2b, recv_z, gat,
           w_s, ex_s, ex_r, c_s, c_r, p_s, p_r, z_s, z_r, az_s, az_r, ap_s, ap_r, ac_s, ac_r):
    i = lax.axis_index("gx")
    j = lax.axis_index("gy")
    n3 = n_gx // 2
    ny = n_gy // 2
    np_ = 2 * ny
    half = acc.shape[1] // 2
    quarter = half // np_
    pad = rz * n3
    slots = feat.shape[0]
    core = lax.rem(j, 2)
    xb = lax.rem(i, 2)
    yb = j // 2
    me_p = yb * 2 + xb
    k = i // 2

    def shift(di, dj):
        return (lax.rem(i + di + n_gx, n_gx), lax.rem(j + dj + n_gy, n_gy))

    def plane_peer(r):
        rx, ry = r % 2, r // 2
        px = lax.rem(xb + rx, 2)
        py = lax.rem(yb + ry, ny)
        return (k * 2 + px, py * 2 + core), py * 2 + px

    def z_peer(d):
        pk = lax.rem(k + d, n3)
        return (pk * 2 + xb, j), pk

    other = (i, yb * 2 + (1 - core))
    dirs = [(a, b) for a in (-1, 0, 1) for b in (-1, 0, 1) if (a, b) != (0, 0)]

    barrier = pltpu.get_barrier_semaphore()
    targets = [shift(a, b) for a, b in dirs] + [other]
    targets += [plane_peer(r)[0] for r in range(1, np_)]
    targets += [z_peer(d)[0] for d in range(1, n3)]
    for t in targets:
        pl.semaphore_signal(barrier, inc=1, device_id=t, device_id_type=MESH)
    load_one = pltpu.make_async_copy(w1_any, w1, w_s.at[0])
    load_two = pltpu.make_async_copy(w2_any, w2, w_s.at[1])
    load_one.start()
    load_two.start()

    def remote(src, dst, ss, rs, dev):
        c = pltpu.make_async_remote_copy(src_ref=src, dst_ref=dst, send_sem=ss, recv_sem=rs,
                                         device_id=dev, device_id_type=MESH)
        c.start()
        return c

    def rows_at(shape, dim):
        row = lax.broadcasted_iota(jnp.int32, shape, dim)
        slot = row >> 6
        inner = ((row >> 4) & 3) * PLANE + (row & 3) * 8 + ((row >> 2) & 3)
        at = jnp.full(shape, -1, jnp.int32)
        for s in range(slots // 64):
            p = pos[s]
            third = (p * 86) >> 8
            corner = (third >> 1) * (4 * PLANE) + (p - 3 * third) * 32 + (third & 1) * 4
            corner = jnp.where(p >= 0, corner, -4 * GRID)
            at = jnp.where(slot == s, corner + inner, at)
        return at

    def one_hot(hit):
        return jnp.where(hit, 1.0, 0.0).astype(BF)

    place = one_hot(lax.broadcasted_iota(jnp.int32, (GRID, slots), 0) == rows_at((1, slots), 1))
    f_row = lax.broadcasted_iota(jnp.int32, (256, 1), 0)
    f_at = ((f_row >> 4) & 7) * PLANE + (f_row & 15) * 8 + (f_row >> 7) * 7
    f_at = jnp.where((f_row & 15) < 12, f_at, -1)
    face = one_hot(lax.broadcasted_iota(jnp.int32, (256, GRID), 1) == f_at)

    def put(f, a):
        gp[f] = a.astype(BF)
        yf[f] = dot(face, gp[f]).astype(BF)

    def exchange(e):
        copies = []
        for n, (a, b) in enumerate(dirs):
            if b == 0:
                src = gp.at[e, pl.ds(0 if a < 0 else GRID - PLANE, PLANE)]
                dst = xr.at[e, 1 if a < 0 else 0]
            else:
                base = 0 if b < 0 else 128
                side = 1 if b < 0 else 0
                if a == 0:
                    src = yf.at[e, pl.ds(base, 128)]
                    dst = yr.at[e, side, pl.ds(16, 128)]
                else:
                    src = yf.at[e, pl.ds(base + (0 if a < 0 else 112), 16)]
                    dst = yr.at[e, side, pl.ds(144 if a < 0 else 0, 16)]
            copies.append(remote(src, dst, ex_s.at[e, n], ex_r.at[e, n], shift(a, b)))
        return copies

    one = jnp.float32(1.0)
    zero = jnp.float32(0.0)
    lo_x = jnp.where(i > 0, one, zero)
    hi_x = jnp.where(i < n_gx - 1, one, zero)
    lo_y = jnp.where(j > 0, one, zero)
    hi_y = jnp.where(j < n_gy - 1, one, zero)

    def build(dst, e, copies):
        for c in copies:
            c.wait_recv()
        row = lax.broadcasted_iota(jnp.int32, (160, C), 0)
        edge = jnp.where(row < 16, lo_x, jnp.where(row >= 144, hi_x, one))
        ylo = dot(spread[0], (yr[e, 0].astype(F32) * (edge * lo_y)).astype(BF))
        yhi = dot(spread[1], (yr[e, 1].astype(F32) * (edge * hi_y)).astype(BF))
        xlo = xr[e, 0].astype(F32) * lo_x
        xhi = xr[e, 1].astype(F32) * hi_x
        ext = jnp.concatenate([xlo, gp[e].astype(F32), xhi], axis=0)
        ypos = lax.broadcasted_iota(jnp.int32, (EXT, C), 0) & 7
        below = jnp.where(ypos == 0, ylo, pltpu.roll(ext, 1, 0))
        above = jnp.where(ypos == 7, yhi, pltpu.roll(ext, EXT - 1, 0))
        blank = jnp.zeros((10, 8, C), F32)
        for dy, v in enumerate((below, ext, above)):
            v = v.reshape(10, PLANE, C)
            forms = (jnp.concatenate([blank, v[:, :PLANE - 8]], axis=1), v,
                     jnp.concatenate([v[:, 8:], blank], axis=1))
            for dz, w in enumerate(forms):
                o = (3 * dy + dz) * C
                dst[:, o:o + C] = w.reshape(EXT, C).astype(BF)

    def conv(f9, w):
        total = None
        for dx in range(3):
            t = dot(f9[dx * PLANE:dx * PLANE + GRID, :], w[dx * TAPS:(dx + 1) * TAPS, :])
            total = t if total is None else total + t
        return total

    def conv_t(f9, wt):
        total = None
        for dx in range(3):
            t = dot_nt(f9[dx * PLANE:dx * PLANE + GRID, :], wt[:, dx * TAPS:(dx + 1) * TAPS])
            total = t if total is None else total + t
        return total

    def core_start(g, left, f9):
        dx = g % 3
        t = dot(left, f9[dx * PLANE:dx * PLANE + GRID, :])
        for q in range(9):
            at = (8 - q if g < 3 else q) * C
            acc[g, at:at + C, :] = t[:, q * C:(q + 1) * C]
        send_c[g] = acc[g, pl.ds(pl.multiple_of((1 - core) * half, 16), half), :].astype(BF)
        return [remote(send_c.at[g], recv_c.at[g], c_s.at[g], c_r.at[g], other)]

    def plane_start(g):
        own = acc[g, pl.ds(pl.multiple_of(core * half, 16), half), :] + recv_c[g].astype(F32)
        s1b[g] = own.astype(BF)
        acc[g, pl.ds(pl.multiple_of(core * half, 16), half), :] = own
        copies = []
        for r in range(1, np_):
            dev, pq = plane_peer(r)
            copies.append(remote(s1b.at[g, pl.ds(pl.multiple_of(pq * quarter, 16), quarter)],
                                 recv_p.at[g, r - 1], p_s.at[g, r - 1], p_r.at[g, r - 1], dev))
        return copies

    def z_start(g):
        at = pl.multiple_of(core * half + me_p * quarter, 16)
        own = acc[g, pl.ds(at, quarter), :]
        for r in range(np_ - 1):
            own = own + recv_p[g, r].astype(F32)
        if pad > quarter:
            own = jnp.concatenate([own, jnp.zeros((pad - quarter, C), F32)], axis=0)
        s2f[g] = own
        s2b[g] = own.astype(BF)
        copies = []
        for d in range(1, n3):
            dev, pk = z_peer(d)
            copies.append(remote(s2b.at[g, pl.ds(pl.multiple_of(pk * rz, 16), rz)],
                                 recv_z.at[g, d - 1], z_s.at[g, d - 1], z_r.at[g, d - 1], dev))
        return copies

    def gather_z(g):
        own = s2f[g, pl.ds(pl.multiple_of(k * rz, 16), rz), :]
        for d in range(n3 - 1):
            own = own + recv_z[g, d].astype(F32)
        at = pl.multiple_of(k * rz, 16)
        gat[g, core * np_ + me_p, pl.ds(at, rz), :] = own.astype(BF)
        block = gat.at[g, core * np_ + me_p, pl.ds(at, rz)]
        return [remote(block, block, az_s.at[g, d - 1], az_r.at[g, d - 1], z_peer(d)[0])
                for d in range(1, n3)]

    def gather_plane(g):
        block = gat.at[g, core * np_ + me_p, pl.ds(0, quarter)]
        return [remote(block, block, ap_s.at[g, r - 1], ap_r.at[g, r - 1], plane_peer(r)[0])
                for r in range(1, np_)]

    def gather_core(g):
        block = gat.at[g, pl.ds(core * np_, np_), pl.ds(0, quarter)]
        return [remote(block, block, ac_s.at[g], ac_r.at[g], other)]

    def finish(g):
        if g < 3:
            first = (18 - 9 * g) * C
            for q in range(2 * np_):
                at = first + q * quarter
                grad_ref[0, at:at + quarter, :] = gat[g, q, 0:quarter, :]
        else:
            first = 9 * (g - 3) * C
            whole = jnp.concatenate([gat[g, q, 0:quarter, :] for q in range(2 * np_)], axis=0)
            for q in range(9):
                block = jnp.transpose(whole[q * C:(q + 1) * C, :].astype(F32))
                grad_ref[1, first + q * C:first + (q + 1) * C, :] = block.astype(BF)
        return []

    stages = (None, plane_start, z_start, gather_z, gather_plane, gather_core, finish)
    flight = {}
    pending = []

    def advance(*steps):
        for stage, g in steps:
            for c in flight[g]:
                c.wait_recv()
            flight[g] = stages[stage](g)
            pending.extend(flight[g])

    def begin(g, left, f9):
        flight[g] = core_start(g, left, f9)
        pending.extend(flight[g])

    xg = dot(place, feat[...])
    put(0, xg)
    pl.semaphore_wait(barrier, len(targets))
    ex_x = exchange(0)
    ug = dot(place, cot[...])
    put(1, ug)
    ex_u = exchange(1)
    mask = dot(place, jnp.ones((slots, C), BF))
    s_col = lax.broadcasted_iota(jnp.int32, (1, 160), 1)
    s_at = jnp.where((s_col & 15) < 12, (s_col >> 4) * PLANE + (s_col & 15) * 8, -8)
    s_row = lax.broadcasted_iota(jnp.int32, (EXT, 160), 0)
    spread[0] = one_hot(s_row == s_at)
    spread[1] = one_hot(s_row == s_at + 7)
    load_one.wait()
    load_two.wait()
    for o in range(27):
        lanes = slice(o * C, (o + 1) * C)
        rows = slice((26 - o) * C, (27 - o) * C)
        wt1[:, lanes] = w1[rows, :]
        wt2[:, lanes] = w2[rows, :]
    build(fx, 0, ex_x)
    pre = conv(fx, w1)
    sig = jax.nn.sigmoid(pre)
    hidden = pre * sig * mask
    h_t = jnp.transpose(hidden).astype(BF)
    build(fu, 1, ex_u)
    for g in range(3):
        begin(g, h_t, fu)
    put(2, hidden)
    advance((1, 0))
    back = conv_t(fu, wt2)
    hgrad = back * (sig * (1.0 + pre * (1.0 - sig))) * mask
    hg_t = jnp.transpose(hgrad).astype(BF)
    advance((1, 1), (1, 2))
    for g in range(3, 6):
        begin(g, hg_t, fx)
    put(3, hgrad)
    ex_h = exchange(2)
    advance((1, 3))
    ex_g = exchange(3)
    advance((2, 0), (1, 4), (1, 5), (2, 1))
    build(fh, 2, ex_h)
    advance((2, 2), (3, 0))
    pre_two = conv(fh, w2)
    advance((3, 1), (2, 3))
    pick = one_hot(lax.broadcasted_iota(jnp.int32, (slots, GRID), 1) == rows_at((slots, 1), 0))
    og = (pre_two + gp[0].astype(F32)).astype(BF)
    out_ref[...] = dot(pick, og).astype(BF)
    advance((3, 2), (4, 0), (2, 4))
    build(fg, 3, ex_g)
    advance((4, 1), (2, 5), (3, 3))
    ig = conv_t(fg, wt1) + gp[1].astype(F32)
    advance((4, 2), (3, 4), (5, 0), (3, 5))
    ig_hi = ig.astype(BF)
    ig_lo = (ig - ig_hi.astype(F32)).astype(BF)
    ig_ref[...] = dot(pick, ig_hi) + dot(pick, ig_lo)
    advance((4, 3), (5, 1), (4, 4), (5, 2), (4, 5), (6, 0), (6, 1), (6, 2), (5, 3), (5, 4), (5, 5),
            (6, 3), (6, 4), (6, 5))
    for c in ex_x + ex_u + ex_g + ex_h + pending:
        c.wait_send()


def finish_kernel(scale, parts, grads, out, ig, out_ref, ig_ref, one_ref, two_ref,
                  narrow, wide, side_out, side_ig, in_s, out_s, side_s):
    size = grads.shape[1] // parts
    chunks = [(g, q) for q in range(parts) for g in range(2)]
    loads = []
    for n, (g, q) in enumerate(chunks):
        loads.append(pltpu.make_async_copy(
            grads.at[g, pl.ds(q * size, size)], narrow.at[n], in_s.at[n]))
        loads[-1].start()
    sides = [pltpu.make_async_copy(out, side_out, side_s.at[0]),
             pltpu.make_async_copy(ig, side_ig, side_s.at[1])]
    for c in sides:
        c.start()
    ends = []
    for n, (g, q) in enumerate(chunks):
        loads[n].wait()
        wide[n] = narrow[n].astype(F32) * scale
        to = one_ref if g else two_ref
        ends.append(pltpu.make_async_copy(wide.at[n], to.at[pl.ds(q * size, size)], out_s.at[n]))
        ends[-1].start()
    backs = [pltpu.make_async_copy(side_out, out_ref, side_s.at[2]),
             pltpu.make_async_copy(side_ig, ig_ref, side_s.at[3])]
    for a, b in zip(sides, backs):
        a.wait()
        b.start()
    for c in ends + backs:
        c.wait()


def per_device(n_gx, n_gy, features, cotangent, block_pos, weight_one, weight_two):
    rows = features.shape[0]
    n3 = n_gx // 2
    np_ = n_gy
    taps = weight_one.shape[0]
    group = taps // 3
    half = group // 2
    quarter = half // np_
    rz = -(-quarter // (16 * n3)) * 16
    pad = rz * n3
    vm = pl.BlockSpec(memory_space=pltpu.VMEM)
    dma = pltpu.SemaphoreType.DMA
    out, ig, grads = pl.pallas_call(
        functools.partial(kernel, n_gx, n_gy, rz),
        out_shape=(jax.ShapeDtypeStruct((rows, C), BF), jax.ShapeDtypeStruct((rows, C), F32),
                   jax.ShapeDtypeStruct((2, taps, C), BF)),
        in_specs=[pl.BlockSpec(memory_space=pltpu.SMEM), vm, vm,
                  pl.BlockSpec(memory_space=pl.ANY), pl.BlockSpec(memory_space=pl.ANY)],
        out_specs=(vm, vm, vm),
        scratch_shapes=[
            pltpu.VMEM((4, GRID, C), BF),
            pltpu.VMEM((4, 256, C), BF),
            pltpu.VMEM((4, 2, PLANE, C), BF),
            pltpu.VMEM((4, 2, 160, C), BF),
            pltpu.VMEM((EXT, TAPS), BF),
            pltpu.VMEM((EXT, TAPS), BF),
            pltpu.VMEM((EXT, TAPS), BF),
            pltpu.VMEM((EXT, TAPS), BF),
            pltpu.VMEM((taps, C), BF),
            pltpu.VMEM((taps, C), BF),
            pltpu.VMEM((C, taps), BF),
            pltpu.VMEM((C, taps), BF),
            pltpu.VMEM((2, EXT, 160), BF),
            pltpu.VMEM((6, group, C), F32),
            pltpu.VMEM((6, half, C), BF),
            pltpu.VMEM((6, half, C), BF),
            pltpu.VMEM((6, half, C), BF),
            pltpu.VMEM((6, np_ - 1, quarter, C), BF),
            pltpu.VMEM((6, pad, C), F32),
            pltpu.VMEM((6, pad, C), BF),
            pltpu.VMEM((6, n3 - 1, rz, C), BF),
            pltpu.VMEM((6, 2 * np_, pad, C), BF),
            dma((2,)),
            dma((4, 8)), dma((4, 8)),
            dma((6,)), dma((6,)),
            dma((6, np_ - 1)), dma((6, np_ - 1)),
            dma((6, n3 - 1)), dma((6, n3 - 1)),
            dma((6, n3 - 1)), dma((6, n3 - 1)),
            dma((6, np_ - 1)), dma((6, np_ - 1)),
            dma((6,)), dma((6,)),
        ],
        compiler_params=pltpu.CompilerParams(
            collective_id=0, has_side_effects=True, vmem_limit_bytes=56 * 1024 * 1024),
        cost_estimate=pl.CostEstimate(flops=5_000_000_000, bytes_accessed=8_000_000,
                                      transcendentals=200_000),
    )(block_pos, features, cotangent, weight_one, weight_two)
    scale = float(1.0 / np.sqrt(np.float32(rows * n_gx * n_gy)))
    parts = 6
    hbm = pl.BlockSpec(memory_space=pl.ANY)
    return tuple(pl.pallas_call(
        functools.partial(finish_kernel, scale, parts),
        out_shape=(jax.ShapeDtypeStruct((rows, C), BF), jax.ShapeDtypeStruct((rows, C), F32),
                   jax.ShapeDtypeStruct((taps, C), F32), jax.ShapeDtypeStruct((taps, C), F32)),
        in_specs=[hbm] * 3,
        out_specs=(hbm,) * 4,
        scratch_shapes=[
            pltpu.VMEM((2 * parts, taps // parts, C), BF),
            pltpu.VMEM((2 * parts, taps // parts, C), F32),
            pltpu.VMEM((rows, C), BF), pltpu.VMEM((rows, C), F32),
            dma((2 * parts,)), dma((2 * parts,)), dma((4,)),
        ],
        compiler_params=pltpu.CompilerParams(vmem_limit_bytes=56 * 1024 * 1024),
    )(grads, out, ig))


def solution(mesh):
    shape = dict(mesh.shape)
    in_specs = (P(("gx", "gy"), None), P(("gx", "gy"), None), P(("gx", "gy")), P(), P())
    out_specs = (P(("gx", "gy"), None), P(("gx", "gy"), None), P(), P())
    return jax.shard_map(
        functools.partial(per_device, shape["gx"], shape["gy"]),
        mesh=mesh, in_specs=in_specs, out_specs=out_specs, check_vma=False,
    )
```

```python
import functools

import jax
import jax.numpy as jnp
import numpy as np
from jax import lax
from jax.experimental import pallas as pl
from jax.experimental.pallas import tpu as pltpu
from jax.sharding import PartitionSpec as P

PLANE = 96
GRID = 768
EXT = 960
C = 128
TAPS = 9 * C
MESH = pl.DeviceIdType.MESH
BF = jnp.bfloat16
F32 = jnp.float32


def dot(a, b):
    return jnp.dot(a, b, preferred_element_type=F32)


def dot_nt(a, b):
    return lax.dot_general(a, b, (((1,), (1,)), ((), ())), preferred_element_type=F32)


def kernel(n_gx, n_gy, rz, pos, feat, cot, w1_any, w2_any,
           out_ref, ig_ref, grad_ref,
           gp, yf, xr, yr, fx, fu, fh, fg, w1, w2, wt1, wt2, spread, acc, send_c, recv_c, s1b,
           recv_p, s2f, s2b, recv_z, gat,
           w_s, ex_s, ex_r, c_s, c_r, p_s, p_r, z_s, z_r, az_s, az_r, ap_s, ap_r, ac_s, ac_r):
    i = lax.axis_index("gx")
    j = lax.axis_index("gy")
    n3 = n_gx // 2
    ny = n_gy // 2
    np_ = 2 * ny
    half = acc.shape[1] // 2
    quarter = half // np_
    pad = rz * n3
    slots = feat.shape[0]
    core = lax.rem(j, 2)
    xb = lax.rem(i, 2)
    yb = j // 2
    me_p = yb * 2 + xb
    k = i // 2

    def shift(di, dj):
        return (lax.rem(i + di + n_gx, n_gx), lax.rem(j + dj + n_gy, n_gy))

    def plane_peer(r):
        rx, ry = r % 2, r // 2
        px = lax.rem(xb + rx, 2)
        py = lax.rem(yb + ry, ny)
        return (k * 2 + px, py * 2 + core), py * 2 + px

    def z_peer(d):
        pk = lax.rem(k + d, n3)
        return (pk * 2 + xb, j), pk

    other = (i, yb * 2 + (1 - core))
    dirs = [(a, b) for a in (-1, 0, 1) for b in (-1, 0, 1) if (a, b) != (0, 0)]

    barrier = pltpu.get_barrier_semaphore()
    targets = [shift(a, b) for a, b in dirs] + [other]
    targets += [plane_peer(r)[0] for r in range(1, np_)]
    targets += [z_peer(d)[0] for d in range(1, n3)]
    for t in targets:
        pl.semaphore_signal(barrier, inc=1, device_id=t, device_id_type=MESH)
    load_one = pltpu.make_async_copy(w1_any, w1, w_s.at[0])
    load_two = pltpu.make_async_copy(w2_any, w2, w_s.at[1])
    load_one.start()
    load_two.start()

    def remote(src, dst, ss, rs, dev):
        c = pltpu.make_async_remote_copy(src_ref=src, dst_ref=dst, send_sem=ss, recv_sem=rs,
                                         device_id=dev, device_id_type=MESH)
        c.start()
        return c

    def rows_at(shape, dim):
        row = lax.broadcasted_iota(jnp.int32, shape, dim)
        slot = row >> 6
        inner = ((row >> 4) & 3) * PLANE + (row & 3) * 8 + ((row >> 2) & 3)
        at = jnp.full(shape, -1, jnp.int32)
        for s in range(slots // 64):
            p = pos[s]
            third = (p * 86) >> 8
            corner = (third >> 1) * (4 * PLANE) + (p - 3 * third) * 32 + (third & 1) * 4
            corner = jnp.where(p >= 0, corner, -4 * GRID)
            at = jnp.where(slot == s, corner + inner, at)
        return at

    def one_hot(hit):
        return jnp.where(hit, 1.0, 0.0).astype(BF)

    place = one_hot(lax.broadcasted_iota(jnp.int32, (GRID, slots), 0) == rows_at((1, slots), 1))
    f_row = lax.broadcasted_iota(jnp.int32, (256, 1), 0)
    f_at = ((f_row >> 4) & 7) * PLANE + (f_row & 15) * 8 + (f_row >> 7) * 7
    f_at = jnp.where((f_row & 15) < 12, f_at, -1)
    face = one_hot(lax.broadcasted_iota(jnp.int32, (256, GRID), 1) == f_at)

    def put(f, a):
        gp[f] = a.astype(BF)
        yf[f] = dot(face, gp[f]).astype(BF)

    def exchange(e):
        copies = []
        for n, (a, b) in enumerate(dirs):
            if b == 0:
                src = gp.at[e, pl.ds(0 if a < 0 else GRID - PLANE, PLANE)]
                dst = xr.at[e, 1 if a < 0 else 0]
            else:
                base = 0 if b < 0 else 128
                side = 1 if b < 0 else 0
                if a == 0:
                    src = yf.at[e, pl.ds(base, 128)]
                    dst = yr.at[e, side, pl.ds(16, 128)]
                else:
                    src = yf.at[e, pl.ds(base + (0 if a < 0 else 112), 16)]
                    dst = yr.at[e, side, pl.ds(144 if a < 0 else 0, 16)]
            copies.append(remote(src, dst, ex_s.at[e, n], ex_r.at[e, n], shift(a, b)))
        return copies

    one = jnp.float32(1.0)
    zero = jnp.float32(0.0)
    lo_x = jnp.where(i > 0, one, zero)
    hi_x = jnp.where(i < n_gx - 1, one, zero)
    lo_y = jnp.where(j > 0, one, zero)
    hi_y = jnp.where(j < n_gy - 1, one, zero)

    def build(dst, e, copies):
        for c in copies:
            c.wait_recv()
        row = lax.broadcasted_iota(jnp.int32, (160, C), 0)
        edge = jnp.where(row < 16, lo_x, jnp.where(row >= 144, hi_x, one))
        ylo = dot(spread[0], (yr[e, 0].astype(F32) * (edge * lo_y)).astype(BF))
        yhi = dot(spread[1], (yr[e, 1].astype(F32) * (edge * hi_y)).astype(BF))
        xlo = xr[e, 0].astype(F32) * lo_x
        xhi = xr[e, 1].astype(F32) * hi_x
        ext = jnp.concatenate([xlo, gp[e].astype(F32), xhi], axis=0)
        ypos = lax.broadcasted_iota(jnp.int32, (EXT, C), 0) & 7
        below = jnp.where(ypos == 0, ylo, pltpu.roll(ext, 1, 0))
        above = jnp.where(ypos == 7, yhi, pltpu.roll(ext, EXT - 1, 0))
        blank = jnp.zeros((10, 8, C), F32)
        for dy, v in enumerate((below, ext, above)):
            v = v.reshape(10, PLANE, C)
            forms = (jnp.concatenate([blank, v[:, :PLANE - 8]], axis=1), v,
                     jnp.concatenate([v[:, 8:], blank], axis=1))
            for dz, w in enumerate(forms):
                o = (3 * dy + dz) * C
                dst[:, o:o + C] = w.reshape(EXT, C).astype(BF)

    def conv(f9, w):
        total = None
        for dx in range(3):
            t = dot(f9[dx * PLANE:dx * PLANE + GRID, :], w[dx * TAPS:(dx + 1) * TAPS, :])
            total = t if total is None else total + t
        return total

    def conv_t(f9, wt):
        total = None
        for dx in range(3):
            t = dot_nt(f9[dx * PLANE:dx * PLANE + GRID, :], wt[:, dx * TAPS:(dx + 1) * TAPS])
            total = t if total is None else total + t
        return total

    def core_start(g, left, f9):
        dx = g % 3
        t = dot(left, f9[dx * PLANE:dx * PLANE + GRID, :])
        for q in range(9):
            at = (8 - q if g < 3 else q) * C
            acc[g, at:at + C, :] = t[:, q * C:(q + 1) * C]
        send_c[g] = acc[g, pl.ds(pl.multiple_of((1 - core) * half, 16), half), :].astype(BF)
        return [remote(send_c.at[g], recv_c.at[g], c_s.at[g], c_r.at[g], other)]

    def plane_start(g):
        own = acc[g, pl.ds(pl.multiple_of(core * half, 16), half), :] + recv_c[g].astype(F32)
        s1b[g] = own.astype(BF)
        acc[g, pl.ds(pl.multiple_of(core * half, 16), half), :] = own
        copies = []
        for r in range(1, np_):
            dev, pq = plane_peer(r)
            copies.append(remote(s1b.at[g, pl.ds(pl.multiple_of(pq * quarter, 16), quarter)],
                                 recv_p.at[g, r - 1], p_s.at[g, r - 1], p_r.at[g, r - 1], dev))
        return copies

    def z_start(g):
        at = pl.multiple_of(core * half + me_p * quarter, 16)
        own = acc[g, pl.ds(at, quarter), :]
        for r in range(np_ - 1):
            own = own + recv_p[g, r].astype(F32)
        if pad > quarter:
            own = jnp.concatenate([own, jnp.zeros((pad - quarter, C), F32)], axis=0)
        s2f[g] = own
        s2b[g] = own.astype(BF)
        copies = []
        for d in range(1, n3):
            dev, pk = z_peer(d)
            copies.append(remote(s2b.at[g, pl.ds(pl.multiple_of(pk * rz, 16), rz)],
                                 recv_z.at[g, d - 1], z_s.at[g, d - 1], z_r.at[g, d - 1], dev))
        return copies

    def gather_z(g):
        own = s2f[g, pl.ds(pl.multiple_of(k * rz, 16), rz), :]
        for d in range(n3 - 1):
            own = own + recv_z[g, d].astype(F32)
        at = pl.multiple_of(k * rz, 16)
        gat[g, core * np_ + me_p, pl.ds(at, rz), :] = own.astype(BF)
        block = gat.at[g, core * np_ + me_p, pl.ds(at, rz)]
        return [remote(block, block, az_s.at[g, d - 1], az_r.at[g, d - 1], z_peer(d)[0])
                for d in range(1, n3)]

    def gather_plane(g):
        block = gat.at[g, core * np_ + me_p, pl.ds(0, quarter)]
        return [remote(block, block, ap_s.at[g, r - 1], ap_r.at[g, r - 1], plane_peer(r)[0])
                for r in range(1, np_)]

    def gather_core(g):
        block = gat.at[g, pl.ds(core * np_, np_), pl.ds(0, quarter)]
        return [remote(block, block, ac_s.at[g], ac_r.at[g], other)]

    def finish(g):
        if g < 3:
            first = (18 - 9 * g) * C
            for q in range(2 * np_):
                at = first + q * quarter
                grad_ref[0, at:at + quarter, :] = gat[g, q, 0:quarter, :]
        else:
            first = 9 * (g - 3) * C
            whole = jnp.concatenate([gat[g, q, 0:quarter, :] for q in range(2 * np_)], axis=0)
            for q in range(9):
                block = jnp.transpose(whole[q * C:(q + 1) * C, :].astype(F32))
                grad_ref[1, first + q * C:first + (q + 1) * C, :] = block.astype(BF)
        return []

    stages = (None, plane_start, z_start, gather_z, gather_plane, gather_core, finish)
    flight = {}
    pending = []

    def advance(*steps):
        for stage, g in steps:
            for c in flight[g]:
                c.wait_recv()
            flight[g] = stages[stage](g)
            pending.extend(flight[g])

    def begin(g, left, f9):
        flight[g] = core_start(g, left, f9)
        pending.extend(flight[g])

    xg = dot(place, feat[...])
    put(0, xg)
    pl.semaphore_wait(barrier, len(targets))
    ex_x = exchange(0)
    ug = dot(place, cot[...])
    put(1, ug)
    ex_u = exchange(1)
    mask = dot(place, jnp.ones((slots, C), BF))
    s_col = lax.broadcasted_iota(jnp.int32, (1, 160), 1)
    s_at = jnp.where((s_col & 15) < 12, (s_col >> 4) * PLANE + (s_col & 15) * 8, -8)
    s_row = lax.broadcasted_iota(jnp.int32, (EXT, 160), 0)
    spread[0] = one_hot(s_row == s_at)
    spread[1] = one_hot(s_row == s_at + 7)
    load_one.wait()
    load_two.wait()
    for o in range(27):
        lanes = slice(o * C, (o + 1) * C)
        rows = slice((26 - o) * C, (27 - o) * C)
        wt1[:, lanes] = w1[rows, :]
        wt2[:, lanes] = w2[rows, :]
    build(fx, 0, ex_x)
    pre = conv(fx, w1)
    sig = jax.nn.sigmoid(pre)
    hidden = pre * sig * mask
    h_t = jnp.transpose(hidden).astype(BF)
    build(fu, 1, ex_u)
    for g in range(3):
        begin(g, h_t, fu)
    put(2, hidden)
    advance((1, 0))
    back = conv_t(fu, wt2)
    hgrad = back * (sig * (1.0 + pre * (1.0 - sig))) * mask
    hg_t = jnp.transpose(hgrad).astype(BF)
    advance((1, 1), (1, 2))
    begin(3, hg_t, fx)
    begin(4, hg_t, fx)
    advance((1, 3))
    begin(5, hg_t, fx)
    advance((1, 4), (2, 0), (1, 5))
    ex_h = exchange(2)
    put(3, hgrad)
    ex_g = exchange(3)
    advance((2, 1))
    build(fh, 2, ex_h)
    advance((2, 2), (3, 0))
    pre_two = conv(fh, w2)
    advance((3, 1), (2, 3))
    pick = one_hot(lax.broadcasted_iota(jnp.int32, (slots, GRID), 1) == rows_at((slots, 1), 0))
    og = (pre_two + gp[0].astype(F32)).astype(BF)
    out_ref[...] = dot(pick, og).astype(BF)
    advance((3, 2), (4, 0), (2, 4))
    build(fg, 3, ex_g)
    advance((4, 1), (2, 5), (3, 3))
    ig = conv_t(fg, wt1) + gp[1].astype(F32)
    advance((4, 2), (3, 4), (5, 0), (3, 5))
    ig_hi = ig.astype(BF)
    ig_lo = (ig - ig_hi.astype(F32)).astype(BF)
    ig_ref[...] = dot(pick, ig_hi) + dot(pick, ig_lo)
    advance((4, 3), (5, 1), (4, 4), (5, 2), (4, 5), (6, 0), (6, 1), (6, 2), (5, 3), (5, 4), (5, 5),
            (6, 3), (6, 4), (6, 5))
    for c in ex_x + ex_u + ex_g + ex_h + pending:
        c.wait_send()


def finish_kernel(scale, parts, grads, out, ig, out_ref, ig_ref, one_ref, two_ref,
                  narrow, wide, side_out, side_ig, in_s, out_s, side_s):
    size = grads.shape[1] // parts
    chunks = [(g, q) for q in range(parts) for g in range(2)]
    loads = []
    for n, (g, q) in enumerate(chunks):
        loads.append(pltpu.make_async_copy(
            grads.at[g, pl.ds(q * size, size)], narrow.at[n], in_s.at[n]))
        loads[-1].start()
    sides = [pltpu.make_async_copy(out, side_out, side_s.at[0]),
             pltpu.make_async_copy(ig, side_ig, side_s.at[1])]
    for c in sides:
        c.start()
    ends = []
    for n, (g, q) in enumerate(chunks):
        loads[n].wait()
        wide[n] = narrow[n].astype(F32) * scale
        to = one_ref if g else two_ref
        ends.append(pltpu.make_async_copy(wide.at[n], to.at[pl.ds(q * size, size)], out_s.at[n]))
        ends[-1].start()
    backs = [pltpu.make_async_copy(side_out, out_ref, side_s.at[2]),
             pltpu.make_async_copy(side_ig, ig_ref, side_s.at[3])]
    for a, b in zip(sides, backs):
        a.wait()
        b.start()
    for c in ends + backs:
        c.wait()


def per_device(n_gx, n_gy, features, cotangent, block_pos, weight_one, weight_two):
    rows = features.shape[0]
    n3 = n_gx // 2
    np_ = n_gy
    taps = weight_one.shape[0]
    group = taps // 3
    half = group // 2
    quarter = half // np_
    rz = -(-quarter // (16 * n3)) * 16
    pad = rz * n3
    vm = pl.BlockSpec(memory_space=pltpu.VMEM)
    dma = pltpu.SemaphoreType.DMA
    out, ig, grads = pl.pallas_call(
        functools.partial(kernel, n_gx, n_gy, rz),
        out_shape=(jax.ShapeDtypeStruct((rows, C), BF), jax.ShapeDtypeStruct((rows, C), F32),
                   jax.ShapeDtypeStruct((2, taps, C), BF)),
        in_specs=[pl.BlockSpec(memory_space=pltpu.SMEM), vm, vm,
                  pl.BlockSpec(memory_space=pl.ANY), pl.BlockSpec(memory_space=pl.ANY)],
        out_specs=(vm, vm, vm),
        scratch_shapes=[
            pltpu.VMEM((4, GRID, C), BF),
            pltpu.VMEM((4, 256, C), BF),
            pltpu.VMEM((4, 2, PLANE, C), BF),
            pltpu.VMEM((4, 2, 160, C), BF),
            pltpu.VMEM((EXT, TAPS), BF),
            pltpu.VMEM((EXT, TAPS), BF),
            pltpu.VMEM((EXT, TAPS), BF),
            pltpu.VMEM((EXT, TAPS), BF),
            pltpu.VMEM((taps, C), BF),
            pltpu.VMEM((taps, C), BF),
            pltpu.VMEM((C, taps), BF),
            pltpu.VMEM((C, taps), BF),
            pltpu.VMEM((2, EXT, 160), BF),
            pltpu.VMEM((6, group, C), F32),
            pltpu.VMEM((6, half, C), BF),
            pltpu.VMEM((6, half, C), BF),
            pltpu.VMEM((6, half, C), BF),
            pltpu.VMEM((6, np_ - 1, quarter, C), BF),
            pltpu.VMEM((6, pad, C), F32),
            pltpu.VMEM((6, pad, C), BF),
            pltpu.VMEM((6, n3 - 1, rz, C), BF),
            pltpu.VMEM((6, 2 * np_, pad, C), BF),
            dma((2,)),
            dma((4, 8)), dma((4, 8)),
            dma((6,)), dma((6,)),
            dma((6, np_ - 1)), dma((6, np_ - 1)),
            dma((6, n3 - 1)), dma((6, n3 - 1)),
            dma((6, n3 - 1)), dma((6, n3 - 1)),
            dma((6, np_ - 1)), dma((6, np_ - 1)),
            dma((6,)), dma((6,)),
        ],
        compiler_params=pltpu.CompilerParams(
            collective_id=0, has_side_effects=True, vmem_limit_bytes=56 * 1024 * 1024),
        cost_estimate=pl.CostEstimate(flops=5_000_000_000, bytes_accessed=8_000_000,
                                      transcendentals=200_000),
    )(block_pos, features, cotangent, weight_one, weight_two)
    scale = float(1.0 / np.sqrt(np.float32(rows * n_gx * n_gy)))
    parts = 6
    hbm = pl.BlockSpec(memory_space=pl.ANY)
    return tuple(pl.pallas_call(
        functools.partial(finish_kernel, scale, parts),
        out_shape=(jax.ShapeDtypeStruct((rows, C), BF), jax.ShapeDtypeStruct((rows, C), F32),
                   jax.ShapeDtypeStruct((taps, C), F32), jax.ShapeDtypeStruct((taps, C), F32)),
        in_specs=[hbm] * 3,
        out_specs=(hbm,) * 4,
        scratch_shapes=[
            pltpu.VMEM((2 * parts, taps // parts, C), BF),
            pltpu.VMEM((2 * parts, taps // parts, C), F32),
            pltpu.VMEM((rows, C), BF), pltpu.VMEM((rows, C), F32),
            dma((2 * parts,)), dma((2 * parts,)), dma((4,)),
        ],
        compiler_params=pltpu.CompilerParams(vmem_limit_bytes=56 * 1024 * 1024),
    )(grads, out, ig))


def solution(mesh):
    shape = dict(mesh.shape)
    in_specs = (P(("gx", "gy"), None), P(("gx", "gy"), None), P(("gx", "gy")), P(), P())
    out_specs = (P(("gx", "gy"), None), P(("gx", "gy"), None), P(), P())
    return jax.shard_map(
        functools.partial(per_device, shape["gx"], shape["gy"]),
        mesh=mesh, in_specs=in_specs, out_specs=out_specs, check_vma=False,
    )
```
